32 devices in a mesh: chain: 2 (over y), cell: 4 (over z), col: 4 (over x, core).
Axes of the slice: x: 2, y: 2, z: 4, core: 2. Of those that a mesh axis runs over, the one named last changes fastest.
Arguments:
- grad: float32 [16384, 64], P(('chain', 'cell', 'col')), parts along dimension 0, may hold values from -6 to 6
- near_tiles: bfloat16 [4, 2, 2048, 2048], P('cell', None, 'col'), may hold values from -0.09375 to 0.09375
- tile_count: int32 [4], replicated, may hold values from 1 to 2
- near_offset: int32 [4], replicated, may hold values from -2 to 2, as said below
- far_src: int32 [4, 8], replicated, may hold values from 0 to 3
- far_count: int32 [4], replicated, may hold values from 1 to 8
- far_cores: float32 [4, 8, 64, 64], P('cell'), may hold values from -0.25 to 0.25
- basis_out: bfloat16 [8192, 64], P(('cell', 'col')), may hold values from -0.75 to 0.75
- basis_in: bfloat16 [8192, 64], P(('cell', 'col')), may hold values from -0.125 to 0.125
Outputs:
- step_block: float32 [16384, 64], P(('chain', 'cell', 'col')), parts along dimension 0
The draws below stay inside these ranges and needn't reach their ends.
There are 2 independent parts, one for each index of `chain`. The reference program is written for one: setup_inputs(seed, part) draws one part's arguments, and reference() takes and returns one part's arrays. A program takes and returns all parts, laid end to end along the dimension named above; an argument that names none is the same for every part. Nothing has to cross between parts.
Inputs may be any that keep to these rules, and one draw needn't show every extreme that they name: c + near_offset[c] is a cluster of the chain, and near_offset[c] is never 0.
All inputs are finite; a program needn't handle non-finite values.
Results may differ from the reference program's by a relative error of at most 0.0035.
Values may be sent and summed in bfloat16 or wider, within the bound.
A program may use at most 64 MiB of HBM per device.

```python
import jax
import jax.numpy as jnp
from jax import lax

CLUS = 2048
COLS = 64
RANK = 64
NEAR = 2
FAR = 8
NCLUS = 4
CELLS = 8192


def draw_near_offset(key, part):
    pick = jax.random.randint(key, (NCLUS,), 0, 4)
    table = jnp.array([-2, -1, 1, 2], jnp.int32)
    offset = table[pick]
    index = jnp.arange(NCLUS, dtype=jnp.int32)
    target = index + offset
    outside = (target < 0) | (target >= NCLUS)
    return jnp.where(outside, -offset, offset).astype(jnp.int32)


def with_ends(values, key, low, high):
    longest = values.shape.index(max(values.shape))
    spots = []
    for shift in (0, 1):
        where = [jax.random.randint(jax.random.fold_in(key, axis), (), 0, length) for axis, length in enumerate(values.shape)]
        where[longest] = (where[longest] + shift) % values.shape[longest]
        spots.append(tuple(where))
    return values.at[spots[0]].set(low).at[spots[1]].set(high)


def block_levels(rng, dims, shards, smallest, high):
    def one(axis_at, parts):
        steps = jax.random.uniform(jax.random.fold_in(jax.random.fold_in(rng, 6), axis_at), (parts,), jnp.float32, smallest / len(shards), high / len(shards))
        return jnp.repeat(jnp.exp(steps), dims[axis_at] // parts).reshape((-1,) + (1,) * (len(dims) - axis_at - 1))

    gain = one(*shards[0])
    for cut in shards[1:]:
        gain = gain * one(*cut)
    return gain


def gaussian(own_key, shape, scale, most, shards=(), kind=jnp.bfloat16):
    gain = block_levels(own_key, shape, shards, -0.22, 0.18) if shards else 1.0
    values = jax.random.normal(own_key, shape, jnp.float32) * scale * gain
    return jnp.minimum(jnp.maximum(values, -most), most).astype(kind)


def setup_inputs(seed: int = 0, part: int = 0) -> dict:
    key_of = jax.random.split(jax.random.key(seed), 10)
    part_keys = jax.random.split(jax.random.fold_in(key_of[9], part), 10)
    grad = gaussian(part_keys[0], (CELLS, COLS), 1.0, 6.0, ((0, 16),), jnp.float32)
    near_tiles = gaussian(key_of[1], (NCLUS, NEAR, CLUS, CLUS), (2 * CLUS) ** -0.5, 0.09375, ((0, 4), (2, 4)))
    tile_count = with_ends(jax.random.randint(key_of[2], (NCLUS,), 1, 3), jax.random.fold_in(key_of[2], 1), 1, 2).astype(jnp.int32)
    near_offset = draw_near_offset(jax.random.fold_in(key_of[9], 71), part)
    far_src = with_ends(jax.random.randint(key_of[4], (NCLUS, FAR), 0, NCLUS), jax.random.fold_in(key_of[4], 1), 0, NCLUS - 1).astype(jnp.int32)
    far_count = with_ends(jax.random.randint(key_of[5], (NCLUS,), 1, FAR + 1), jax.random.fold_in(key_of[5], 1), 1, FAR).astype(jnp.int32)
    far_cores = gaussian(key_of[6], (NCLUS, FAR, RANK, RANK), (RANK * FAR) ** -0.5, 0.25, ((0, 4),), jnp.float32)
    basis_out = gaussian(key_of[7], (CELLS, RANK), RANK ** -0.5, 0.75, ((0, 16),))
    basis_in = gaussian(key_of[8], (CELLS, RANK), CLUS ** -0.5, 0.125, ((0, 16),))
    return {"grad": grad, "near_tiles": near_tiles, "tile_count": tile_count, "near_offset": near_offset, "far_src": far_src, "far_count": far_count, "far_cores": far_cores, "basis_out": basis_out, "basis_in": basis_in}


def reference(grad, near_tiles, tile_count, near_offset, far_src, far_count, far_cores, basis_out, basis_in):
    rounded = grad.astype(jnp.bfloat16).reshape(NCLUS, CLUS, COLS)
    inbasis = basis_in.reshape(NCLUS, CLUS, RANK)
    outbasis = basis_out.reshape(NCLUS, CLUS, RANK)
    proj = jnp.einsum("cra,crw->caw", inbasis.astype(jnp.float32), rounded.astype(jnp.float32), precision=lax.Precision.HIGHEST)
    slots = jnp.arange(FAR, dtype=jnp.int32)

    def one_cluster(index):
        tiles = near_tiles[index]
        own = jnp.dot(tiles[0], rounded[index], preferred_element_type=jnp.float32)
        source = (index + near_offset[index]).astype(jnp.int32)
        other = jnp.dot(tiles[1], rounded[source], preferred_element_type=jnp.float32)
        near = own + jnp.where(tile_count[index] == 2, other, jnp.zeros_like(other))
        picked = proj[far_src[index]]
        cores = jnp.where((slots < far_count[index])[:, None, None], far_cores[index], jnp.zeros_like(far_cores[index]))
        coupled = jnp.einsum("kab,kbw->aw", cores, picked, precision=lax.Precision.HIGHEST)
        far = jnp.dot(outbasis[index], coupled.astype(jnp.bfloat16), preferred_element_type=jnp.float32)
        return near + far

    result = lax.map(one_cluster, jnp.arange(NCLUS, dtype=jnp.int32))
    return result.reshape(NCLUS * CLUS, COLS)
```

```python
import functools

import jax
import jax.numpy as jnp
from jax import lax
from jax.experimental import pallas as pl
from jax.experimental.pallas import tpu as pltpu
from jax.sharding import PartitionSpec as P

MESH = pl.DeviceIdType.MESH
OFFSETS = (-2, -1, 1, 2)
F32 = jnp.float32
BF16 = jnp.bfloat16


def remote(src, dst, send, recv, **where):
    return pltpu.make_async_remote_copy(
        src_ref=src, dst_ref=dst, send_sem=send, recv_sem=recv, device_id=where, device_id_type=MESH
    )


def kernel(
    n_cell, n_col,
    count_ref, offset_ref, fsrc_ref, fcount_ref, grad_hbm, tiles_hbm, cores_hbm, bout_hbm, bin_hbm,
    out_ref,
    grad, tiles, cores, bout, bin_,
    own, near, beside, ppt, part, table, coret, acc,
    local_sem, own_send, own_recv, near_send, near_recv, side_send, side_recv,
    part_send, part_recv, table_send, table_recv, core_send, core_recv,
):
    cell = lax.axis_index("cell")
    col = lax.axis_index("col")
    rows = grad.shape[0]
    half = rows // 2
    width = grad.shape[1]
    piece = width // n_col
    bits = [1 << b for b in reversed(range(n_col.bit_length() - 1))]

    def flip(d):
        value = col
        for b in bits:
            if d & b:
                value = value + b - 2 * b * lax.rem(value // b, 2)
        return value

    barrier = pltpu.get_barrier_semaphore()
    for d in range(1, n_col):
        pl.semaphore_signal(barrier, inc=1, device_id={"col": flip(d)}, device_id_type=MESH)
    for d in range(1, n_cell):
        pl.semaphore_signal(
            barrier, inc=1, device_id={"cell": lax.rem(cell + d, n_cell)}, device_id_type=MESH
        )

    loads = [
        pltpu.make_async_copy(src, dst, local_sem.at[i])
        for i, (src, dst) in enumerate((
            (grad_hbm, grad), (bin_hbm, bin_), (tiles_hbm.at[0, 0], tiles.at[0]),
            (cores_hbm.at[0], cores), (bout_hbm, bout), (tiles_hbm.at[0, 1], tiles.at[1]),
        ))
    ]
    for load in loads:
        load.start()

    loads[0].wait()
    rounded = grad[...].astype(BF16)
    own[col] = jnp.concatenate([rounded[:half], rounded[half:]], axis=1)
    loads[1].wait()
    ppt[...] = lax.dot_general(rounded, bin_[...], (((0,), (0,)), ((), ())), preferred_element_type=F32)
    for p, step in enumerate(OFFSETS):
        @pl.when((cell + step < 0) | (cell + step >= n_cell))
        def _():
            near[p] = jnp.zeros(near.shape[1:], BF16)

    pl.semaphore_wait(barrier, (n_col - 1) + (n_cell - 1))

    part_copies = [
        remote(ppt.at[pl.ds(pl.multiple_of(flip(d) * piece, piece), piece)], part.at[d - 1],
               part_send.at[d - 1], part_recv.at[d - 1], col=flip(d))
        for d in range(1, n_col)
    ]
    for copy in part_copies:
        copy.start()

    near_copies = []
    for p, step in enumerate(OFFSETS):
        target = cell - step
        near_copies.append(remote(
            own.at[col], near.at[p], near_send.at[p], near_recv.at[p],
            cell=jnp.clip(target, 0, n_cell - 1)))
    for p in (0, 3, 1, 2):
        step = OFFSETS[p]
        @pl.when((cell - step >= 0) & (cell - step < n_cell))
        def _():
            near_copies[p].start()

    def cube(buf, send, recv):
        copies, index, held = {}, 0, [0]
        for b in bits:
            for h in list(held):
                slot = flip(h)
                copies[h, b] = remote(buf.at[slot], buf.at[slot], send.at[index], recv.at[index], col=flip(b))
                index += 1
            held += [h ^ b for h in held]
        return copies

    own_copies = cube(own, own_send, own_recv)
    side_copies = cube(beside, side_send, side_recv)

    def begin(copies, h):
        for (held, b), copy in copies.items():
            if held == h:
                copy.start()

    def arrive(copies, h):
        for (held, b), copy in copies.items():
            if held ^ b == h:
                copy.wait_recv()

    def forward_order():
        held = [0]
        for b in bits:
            held += [h ^ b for h in held]
        return held

    order = forward_order()

    begin(own_copies, 0)

    for copy in part_copies:
        copy.wait_recv()
    total = ppt[pl.ds(pl.multiple_of(col * piece, piece), piece), :]
    for d in range(1, n_col):
        total = total + part[d - 1]
    table[cell] = total
    table_copies = [
        remote(table.at[cell], table.at[cell], table_send.at[d - 1], table_recv.at[d - 1],
               cell=lax.rem(cell + d, n_cell))
        for d in range(1, n_cell)
    ]
    for copy in table_copies:
        copy.start()

    def product(tile, buf, slot):
        block = buf[slot]
        for h in range(2):
            columns = pl.ds(pl.multiple_of(slot * rows + h * half, half), half)
            acc[h] += jnp.dot(tiles[tile, :, columns], block, preferred_element_type=F32)

    loads[2].wait()
    acc[...] = jnp.zeros_like(acc)
    product(0, own, col)
    for h in order[1:]:
        arrive(own_copies, h)
        begin(own_copies, h)
        if h == bits[0]:
            for p, step in enumerate(OFFSETS):
                @pl.when((cell + step >= 0) & (cell + step < n_cell))
                def _():
                    near_copies[p].wait_recv()
            offset = offset_ref[cell]
            position = offset + 2 - (offset > 0).astype(jnp.int32)
            picked = near[position]
            beside[col] = jnp.where(count_ref[cell] == 2, picked, jnp.zeros_like(picked))
            begin(side_copies, 0)
        product(0, own, flip(h))

    for copy in table_copies:
        copy.wait_recv()
    loads[3].wait()
    used = fcount_ref[cell]
    mixed = jnp.zeros((piece, width), F32)
    for k in range(cores.shape[0]):
        source = table[fsrc_ref[cell, k]]
        source = jnp.where(k < used, source, jnp.zeros_like(source))
        mixed = mixed + lax.dot_general(
            source, cores[k], (((1,), (1,)), ((), ())),
            precision=lax.Precision.HIGHEST, preferred_element_type=F32)
    mine = pl.ds(pl.multiple_of(col * piece, piece), piece)
    coret[mine, :] = mixed.astype(BF16)
    core_copies = [
        remote(coret.at[mine], coret.at[mine], core_send.at[d - 1], core_recv.at[d - 1], col=flip(d))
        for d in range(1, n_col)
    ]
    for copy in core_copies:
        copy.start()

    loads[5].wait()
    product(1, beside, col)
    for h in order[1:]:
        arrive(side_copies, h)
        begin(side_copies, h)
        product(1, beside, flip(h))

    loads[4].wait()
    for copy in core_copies:
        copy.wait_recv()
    far = lax.dot_general(bout[...], coret[...], (((1,), (1,)), ((), ())), preferred_element_type=F32)
    out_ref[...] = acc[0][:, :width] + acc[1][:, width:] + far

    for copy in part_copies + table_copies + core_copies:
        copy.wait_send()
    for copy in list(own_copies.values()) + list(side_copies.values()):
        copy.wait_send()
    for p, step in enumerate(OFFSETS):
        @pl.when((cell - step >= 0) & (cell - step < n_cell))
        def _():
            near_copies[p].wait_send()


def body(
    n_cell, n_col,
    grad, near_tiles, tile_count, near_offset, far_src, far_count, far_cores, basis_out, basis_in
):
    rows, width = grad.shape
    slots, _, clus = near_tiles.shape[1:]
    far, rank = far_cores.shape[1:3]
    half, piece = rows // 2, width // n_col
    dma = lambda n: pltpu.SemaphoreType.DMA((max(n, 1),))
    smem = pl.BlockSpec(memory_space=pltpu.SMEM)
    anywhere = pl.BlockSpec(memory_space=pl.ANY)
    return pl.pallas_call(
        functools.partial(kernel, n_cell, n_col),
        out_shape=jax.ShapeDtypeStruct((rows, width), F32),
        in_specs=[smem] * 4 + [anywhere] * 5,
        out_specs=pl.BlockSpec(memory_space=pltpu.VMEM),
        scratch_shapes=[
            pltpu.VMEM((rows, width), F32),
            pltpu.VMEM((slots, rows, clus), BF16),
            pltpu.VMEM((far, rank, rank), F32),
            pltpu.VMEM((rows, rank), BF16),
            pltpu.VMEM((rows, rank), BF16),
            pltpu.VMEM((n_col, half, 2 * width), BF16),
            pltpu.VMEM((len(OFFSETS), half, 2 * width), BF16),
            pltpu.VMEM((n_col, half, 2 * width), BF16),
            pltpu.VMEM((width, rank), F32),
            pltpu.VMEM((n_col - 1, piece, rank), F32),
            pltpu.VMEM((n_cell, piece, rank), F32),
            pltpu.VMEM((width, rank), BF16),
            pltpu.VMEM((2, rows, 2 * width), F32),
            dma(6),
            dma(n_col - 1), dma(n_col - 1),
            dma(len(OFFSETS)), dma(len(OFFSETS)),
            dma(n_col - 1), dma(n_col - 1),
            dma(n_col - 1), dma(n_col - 1),
            dma(n_cell - 1), dma(n_cell - 1),
            dma(n_col - 1), dma(n_col - 1),
        ],
        compiler_params=pltpu.CompilerParams(
            collective_id=0, has_side_effects=True, vmem_limit_bytes=48 * 1024 * 1024
        ),
    )(tile_count, near_offset, far_src, far_count, grad, near_tiles, far_cores, basis_out, basis_in)


def solution(mesh):
    placed = (
        P(("chain", "cell", "col"), None),
        P("cell", None, "col", None),
        P(),
        P(),
        P(),
        P(),
        P("cell", None, None, None),
        P(("cell", "col"), None),
        P(("cell", "col"), None),
    )
    return jax.shard_map(
        functools.partial(body, mesh.shape["cell"], mesh.shape["col"]),
        mesh=mesh,
        in_specs=placed,
        out_specs=P(("chain", "cell", "col"), None),
        check_vma=False,
    )
```

```python
import functools

import jax
import jax.numpy as jnp
from jax import lax
from jax.experimental import pallas as pl
from jax.experimental.pallas import tpu as pltpu
from jax.sharding import PartitionSpec as P

MESH = pl.DeviceIdType.MESH
OFFSETS = (-2, -1, 1, 2)
CHUNKS = 2
F32 = jnp.float32
BF16 = jnp.bfloat16


def remote(src, dst, send, recv, **where):
    return pltpu.make_async_remote_copy(
        src_ref=src, dst_ref=dst, send_sem=send, recv_sem=recv, device_id=where, device_id_type=MESH
    )


def across(a, b, **kw):
    return lax.dot_general(a, b, (((1,), (1,)), ((), ())), preferred_element_type=F32, **kw)


def kernel(
    n_cell, n_col,
    count_hbm, offset_hbm, fsrc_hbm, fcount_hbm, grad_hbm, tiles_hbm, cores_hbm, bout_hbm, bin_hbm,
    out_ref,
    count_ref, offset_ref, fsrc_ref, fcount_ref,
    grad, tiles, cores, bout, bin_,
    own, near, beside, ppt, part, table, flat, coret, acc,
    local_sem, own_send, own_recv, near_send, near_recv, side_send, side_recv,
    part_send, part_recv, table_send, table_recv, core_send, core_recv,
):
    cell = lax.axis_index("cell")
    col = lax.axis_index("col")
    width, rows = grad.shape
    size = rows // CHUNKS
    piece = width // n_col
    bits = [1 << b for b in reversed(range(n_col.bit_length() - 1))]

    def flip(d):
        value = col
        for b in bits:
            if d & b:
                value = value + b - 2 * b * lax.rem(value // b, 2)
        return value

    barrier = pltpu.get_barrier_semaphore()
    for d in range(1, n_col):
        pl.semaphore_signal(barrier, inc=1, device_id={"col": flip(d)}, device_id_type=MESH)
    for d in range(1, n_cell):
        pl.semaphore_signal(
            barrier, inc=1, device_id={"cell": lax.rem(cell + d, n_cell)}, device_id_type=MESH
        )

    pairs = {
        "grad": (grad_hbm, grad), "bin": (bin_hbm, bin_),
        "count": (count_hbm, count_ref), "offset": (offset_hbm, offset_ref),
        "fsrc": (fsrc_hbm, fsrc_ref), "fcount": (fcount_hbm, fcount_ref),
        "cores": (cores_hbm.at[0], cores), "tile0": (tiles_hbm.at[0, 0], tiles.at[0]),
        "bout": (bout_hbm, bout), "tile1": (tiles_hbm.at[0, 1], tiles.at[1]),
    }
    loads = {
        name: pltpu.make_async_copy(src, dst, local_sem.at[i])
        for i, (name, (src, dst)) in enumerate(pairs.items())
    }
    for load in loads.values():
        load.start()

    loads["grad"].wait()
    rounded = grad[...].astype(BF16)
    for q in range(CHUNKS):
        own[col, q] = rounded[:, q * size:(q + 1) * size]
    loads["bin"].wait()
    ppt[...] = across(rounded, bin_[...])
    for p, step in enumerate(OFFSETS):
        @pl.when((cell + step < 0) | (cell + step >= n_cell))
        def _():
            near[p] = jnp.zeros(near.shape[1:], BF16)
    loads["cores"].wait()
    rank = cores.shape[1]
    for k in range(0, cores.shape[0], 2):
        flat[:, k * rank:(k + 2) * rank] = jnp.concatenate([cores[k], cores[k + 1]], axis=1)
    for name in ("count", "offset", "fsrc", "fcount"):
        loads[name].wait()

    pl.semaphore_wait(barrier, (n_col - 1) + (n_cell - 1))

    part_copies = [
        remote(ppt.at[pl.ds(pl.multiple_of(flip(d) * piece, piece), piece)], part.at[d - 1],
               part_send.at[d - 1], part_recv.at[d - 1], col=flip(d))
        for d in range(1, n_col)
    ]
    for copy in part_copies:
        copy.start()

    near_copies = {}
    for q in range(CHUNKS):
        for p, step in enumerate(OFFSETS):
            index = q * len(OFFSETS) + p
            near_copies[q, p] = remote(
                own.at[col, q], near.at[p, q], near_send.at[index], near_recv.at[index],
                cell=jnp.clip(cell - step, 0, n_cell - 1))
    for q in range(CHUNKS):
        for p in (0, 3, 1, 2):
            step = OFFSETS[p]
            @pl.when((cell - step >= 0) & (cell - step < n_cell))
            def _():
                near_copies[q, p].start()

    def cube(buf, send, recv):
        copies, index, held = {}, 0, [0]
        for b in bits:
            for h in list(held):
                slot = flip(h)
                for q in range(CHUNKS):
                    copies[h, q, b] = remote(
                        buf.at[slot, q], buf.at[slot, q], send.at[index], recv.at[index], col=flip(b))
                    index += 1
            held += [h ^ b for h in held]
        return copies, held

    own_copies, order = cube(own, own_send, own_recv)
    side_copies, _ = cube(beside, side_send, side_recv)

    def begin(copies, h, q):
        for (held, chunk, b), copy in copies.items():
            if held == h and chunk == q:
                copy.start()

    def arrive(copies, h, q):
        for (held, chunk, b), copy in copies.items():
            if held ^ b == h and chunk == q:
                copy.wait_recv()

    for q in range(CHUNKS):
        begin(own_copies, 0, q)

    def product(tile, buf, slot, q):
        columns = pl.ds(pl.multiple_of(slot * rows + q * size, size), size)
        acc[...] += across(buf[slot, q], tiles[tile, :, columns])

    acc[...] = jnp.zeros_like(acc)
    loads["tile0"].wait()
    for q in range(CHUNKS):
        product(0, own, col, q)

    for copy in part_copies:
        copy.wait_recv()
    total = ppt[pl.ds(pl.multiple_of(col * piece, piece), piece), :]
    for d in range(1, n_col):
        total = total + part[d - 1]
    table[cell] = total
    table_copies = [
        remote(table.at[cell], table.at[cell], table_send.at[d - 1], table_recv.at[d - 1],
               cell=lax.rem(cell + d, n_cell))
        for d in range(1, n_cell)
    ]
    for copy in table_copies:
        copy.start()

    for h in order[1:]:
        for q in range(CHUNKS):
            arrive(own_copies, h, q)
            begin(own_copies, h, q)
        if h == bits[0]:
            for q in range(CHUNKS):
                product(0, own, flip(h), q)

    offset = offset_ref[cell]
    position = offset + 2 - (offset > 0).astype(jnp.int32)
    use = count_ref[cell] == 2
    for q in range(CHUNKS):
        for p, step in enumerate(OFFSETS):
            @pl.when((cell + step >= 0) & (cell + step < n_cell))
            def _():
                near_copies[q, p].wait_recv()
        if q == CHUNKS - 1:
            for c in range(CHUNKS):
                picked = near[position, c]
                beside[col, c] = jnp.where(use, picked, jnp.zeros_like(picked))
                begin(side_copies, 0, c)

    for copy in table_copies:
        copy.wait_recv()
    used = fcount_ref[cell]
    picks = []
    for k in range(cores.shape[0]):
        source = table[fsrc_ref[cell, k]]
        picks.append(jnp.where(k < used, source, jnp.zeros_like(source)))
    mixed = across(jnp.concatenate(picks, axis=1), flat[...], precision=lax.Precision.HIGHEST)
    mine = pl.ds(pl.multiple_of(col * piece, piece), piece)
    coret[mine, :] = mixed.astype(BF16)
    core_copies = [
        remote(coret.at[mine], coret.at[mine], core_send.at[d - 1], core_recv.at[d - 1], col=flip(d))
        for d in range(1, n_col)
    ]
    for copy in core_copies:
        copy.start()

    for h in order[1:]:
        if h != bits[0]:
            for q in range(CHUNKS):
                product(0, own, flip(h), q)
    loads["tile1"].wait()
    for q in range(CHUNKS):
        product(1, beside, col, q)
    for h in order[1:]:
        for q in range(CHUNKS):
            arrive(side_copies, h, q)
            begin(side_copies, h, q)
            product(1, beside, flip(h), q)

    loads["bout"].wait()
    for copy in core_copies:
        copy.wait_recv()
    out_ref[...] = acc[...] + jnp.dot(coret[...], bout[...], preferred_element_type=F32)

    for copy in part_copies + table_copies + core_copies:
        copy.wait_send()
    for copy in list(own_copies.values()) + list(side_copies.values()):
        copy.wait_send()
    for q in range(CHUNKS):
        for p, step in enumerate(OFFSETS):
            @pl.when((cell - step >= 0) & (cell - step < n_cell))
            def _():
                near_copies[q, p].wait_send()


def body(
    n_cell, n_col,
    grad, near_tiles, tile_count, near_offset, far_src, far_count, far_cores, basis_out, basis_in
):
    rows, width = grad.shape
    slots, _, clus = near_tiles.shape[1:]
    far, rank = far_cores.shape[1:3]
    size, piece = rows // CHUNKS, width // n_col
    dma = lambda n: pltpu.SemaphoreType.DMA((max(n, 1),))
    hbm = pl.BlockSpec(memory_space=pltpu.HBM)
    out = pl.pallas_call(
        functools.partial(kernel, n_cell, n_col),
        out_shape=jax.ShapeDtypeStruct((width, rows), F32),
        in_specs=[hbm] * 9,
        out_specs=pl.BlockSpec(memory_space=pltpu.VMEM),
        scratch_shapes=[
            pltpu.SMEM(tile_count.shape, jnp.int32),
            pltpu.SMEM(near_offset.shape, jnp.int32),
            pltpu.SMEM(far_src.shape, jnp.int32),
            pltpu.SMEM(far_count.shape, jnp.int32),
            pltpu.VMEM((width, rows), F32),
            pltpu.VMEM((slots, rows, clus), BF16),
            pltpu.VMEM((far, rank, rank), F32),
            pltpu.VMEM((rank, rows), BF16),
            pltpu.VMEM((rank, rows), BF16),
            pltpu.VMEM((n_col, CHUNKS, width, size), BF16),
            pltpu.VMEM((len(OFFSETS), CHUNKS, width, size), BF16),
            pltpu.VMEM((n_col, CHUNKS, width, size), BF16),
            pltpu.VMEM((width, rank), F32),
            pltpu.VMEM((n_col - 1, piece, rank), F32),
            pltpu.VMEM((n_cell, piece, rank), F32),
            pltpu.VMEM((rank, far * rank), F32),
            pltpu.VMEM((width, rank), BF16),
            pltpu.VMEM((width, rows), F32),
            dma(10),
            dma((n_col - 1) * CHUNKS), dma((n_col - 1) * CHUNKS),
            dma(len(OFFSETS) * CHUNKS), dma(len(OFFSETS) * CHUNKS),
            dma((n_col - 1) * CHUNKS), dma((n_col - 1) * CHUNKS),
            dma(n_col - 1), dma(n_col - 1),
            dma(n_cell - 1), dma(n_cell - 1),
            dma(n_col - 1), dma(n_col - 1),
        ],
        compiler_params=pltpu.CompilerParams(
            collective_id=0, has_side_effects=True, vmem_limit_bytes=63 * 1024 * 1024
        ),
    )(tile_count, near_offset, far_src, far_count, grad.T, near_tiles, far_cores, basis_out.T, basis_in.T)
    return out.T


def solution(mesh):
    placed = (
        P(("chain", "cell", "col"), None),
        P("cell", None, "col", None),
        P(),
        P(),
        P(),
        P(),
        P("cell", None, None, None),
        P(("cell", "col"), None),
        P(("cell", "col"), None),
    )
    return jax.shard_map(
        functools.partial(body, mesh.shape["cell"], mesh.shape["col"]),
        mesh=mesh,
        in_specs=placed,
        out_specs=P(("chain", "cell", "col"), None),
        check_vma=False,
    )
```

```python
import functools

import jax
import jax.numpy as jnp
from jax import lax
from jax.experimental import pallas as pl
from jax.experimental.pallas import tpu as pltpu
from jax.sharding import PartitionSpec as P

MESH = pl.DeviceIdType.MESH
OFFSETS = (-2, -1, 1, 2)
CHUNKS = 2
F32 = jnp.float32
BF16 = jnp.bfloat16


def remote(src, dst, send, recv, **where):
    return pltpu.make_async_remote_copy(
        src_ref=src, dst_ref=dst, send_sem=send, recv_sem=recv, device_id=where, device_id_type=MESH
    )


def across(a, b, **kw):
    return lax.dot_general(a, b, (((1,), (1,)), ((), ())), preferred_element_type=F32, **kw)


def kernel(
    n_cell, n_col,
    count_hbm, offset_hbm, fsrc_hbm, fcount_hbm, grad_hbm, tiles_hbm, cores_hbm, bout_hbm, bin_hbm,
    out_ref,
    count_ref, offset_ref, fsrc_ref, fcount_ref,
    grad, tiles, cores, bout, bin_,
    own, near, beside, ppt, part, table, flat, coret, acc,
    local_sem, own_send, own_recv, near_send, near_recv, side_send, side_recv,
    part_send, part_recv, table_send, table_recv, core_send, core_recv,
):
    cell = lax.axis_index("cell")
    col = lax.axis_index("col")
    width, rows = grad.shape
    size = rows // CHUNKS
    piece = width // n_col
    bits = [1 << b for b in reversed(range(n_col.bit_length() - 1))]

    def flip(d):
        value = col
        for b in bits:
            if d & b:
                value = value + b - 2 * b * lax.rem(value // b, 2)
        return value

    barrier = pltpu.get_barrier_semaphore()
    for d in range(1, n_col):
        pl.semaphore_signal(barrier, inc=1, device_id={"col": flip(d)}, device_id_type=MESH)
    for d in range(1, n_cell):
        pl.semaphore_signal(
            barrier, inc=1, device_id={"cell": lax.rem(cell + d, n_cell)}, device_id_type=MESH
        )

    pairs = {
        "grad": (grad_hbm, grad), "bin": (bin_hbm, bin_),
        "count": (count_hbm, count_ref), "offset": (offset_hbm, offset_ref),
        "fsrc": (fsrc_hbm, fsrc_ref), "fcount": (fcount_hbm, fcount_ref),
        "cores": (cores_hbm.at[0], cores), "tile0": (tiles_hbm.at[0, 0], tiles.at[0]),
        "bout": (bout_hbm, bout), "tile1": (tiles_hbm.at[0, 1], tiles.at[1]),
    }
    loads = {
        name: pltpu.make_async_copy(src, dst, local_sem.at[i])
        for i, (name, (src, dst)) in enumerate(pairs.items())
    }
    for name in ("grad", "bin", "count", "offset"):
        loads[name].start()

    for p, step in enumerate(OFFSETS):
        @pl.when((cell + step < 0) | (cell + step >= n_cell))
        def _():
            near[p] = jnp.zeros(near.shape[1:], BF16)
    loads["grad"].wait()
    rounded = grad[...].astype(BF16)
    for q in range(CHUNKS):
        own[col, q] = rounded[:, q * size:(q + 1) * size]

    up, down = jnp.minimum(cell + 1, n_cell - 1), jnp.maximum(cell - 1, 0)
    below, above = cell > 0, cell < n_cell - 1
    inner = below & above
    near_copies, near_when = {}, {}
    for q in range(CHUNKS):
        for p, src, target, when in (
            (0, near.at[1, q], up, inner), (1, own.at[col, q], up, above),
            (2, own.at[col, q], down, below), (3, near.at[2, q], down, inner),
        ):
            index = q * len(OFFSETS) + p
            near_copies[q, p] = remote(
                src, near.at[p, q], near_send.at[index], near_recv.at[index], cell=target)
            near_when[p] = when

    def near_start(q, p):
        pl.when(near_when[p])(near_copies[q, p].start)

    def near_arrive(q, p):
        step = OFFSETS[p]
        pl.when((cell + step >= 0) & (cell + step < n_cell))(near_copies[q, p].wait_recv)

    def cube(buf, send, recv):
        copies, index, held = {}, 0, [0]
        for b in bits:
            for h in list(held):
                slot = flip(h)
                for q in range(CHUNKS):
                    copies[h, q, b] = remote(
                        buf.at[slot, q], buf.at[slot, q], send.at[index], recv.at[index], col=flip(b))
                    index += 1
            held += [h ^ b for h in held]
        return copies, held

    own_copies, order = cube(own, own_send, own_recv)
    side_copies, _ = cube(beside, side_send, side_recv)

    def begin(copies, h, q):
        for (held, chunk, b), copy in copies.items():
            if held == h and chunk == q:
                copy.start()

    def arrive(copies, h, q):
        for (held, chunk, b), copy in copies.items():
            if held ^ b == h and chunk == q:
                copy.wait_recv()

    pl.semaphore_wait(barrier, (n_col - 1) + (n_cell - 1))

    def first(q):
        near_start(q, 1)
        near_start(q, 2)
        begin(own_copies, 0, q)

    first(0)
    loads["bin"].wait()
    ppt[...] = across(rounded, bin_[...])
    part_copies = [
        remote(ppt.at[pl.ds(pl.multiple_of(flip(d) * piece, piece), piece)], part.at[d - 1],
               part_send.at[d - 1], part_recv.at[d - 1], col=flip(d))
        for d in range(1, n_col)
    ]
    for copy in part_copies:
        copy.start()

    for q in range(1, CHUNKS):
        first(q)
    for name in ("tile0", "cores", "fsrc", "fcount", "tile1", "bout"):
        loads[name].start()

    def product(tile, buf, slot, q):
        columns = pl.ds(pl.multiple_of(slot * rows + q * size, size), size)
        acc[...] += across(buf[slot, q], tiles[tile, :, columns])

    acc[...] = jnp.zeros_like(acc)
    for copy in part_copies:
        copy.wait_recv()
    total = ppt[pl.ds(pl.multiple_of(col * piece, piece), piece), :]
    for d in range(1, n_col):
        total = total + part[d - 1]
    table[cell] = total
    table_copies = [
        remote(table.at[cell], table.at[cell], table_send.at[d - 1], table_recv.at[d - 1],
               cell=lax.rem(cell + d, n_cell))
        for d in range(1, n_cell)
    ]
    for copy in table_copies:
        copy.start()

    for q in range(CHUNKS):
        near_arrive(q, 1)
        near_start(q, 0)
        near_arrive(q, 2)
        near_start(q, 3)
    loads["tile0"].wait()
    for q in range(CHUNKS):
        product(0, own, col, q)
    for h in order[1:]:
        for q in range(CHUNKS):
            arrive(own_copies, h, q)
            begin(own_copies, h, q)
        if h == bits[0]:
            for q in range(CHUNKS):
                product(0, own, flip(h), q)

    for name in ("cores", "fsrc", "fcount", "count", "offset"):
        loads[name].wait()
    rank = cores.shape[1]
    for k in range(0, cores.shape[0], 2):
        flat[:, k * rank:(k + 2) * rank] = jnp.concatenate([cores[k], cores[k + 1]], axis=1)

    offset = offset_ref[cell]
    use = count_ref[cell] == 2
    for q in range(CHUNKS):
        near_arrive(q, 0)
        near_arrive(q, 3)
        picked = jnp.zeros(near.shape[2:], BF16)
        for p, step in enumerate(OFFSETS):
            picked = jnp.where(use & (offset == step), near[p, q], picked)
        beside[col, q] = picked
        begin(side_copies, 0, q)

    for copy in table_copies:
        copy.wait_recv()
    used = fcount_ref[cell]
    picks = []
    for k in range(cores.shape[0]):
        source = table[fsrc_ref[cell, k]]
        picks.append(jnp.where(k < used, source, jnp.zeros_like(source)))
    mixed = across(jnp.concatenate(picks, axis=1), flat[...], precision=lax.Precision.HIGHEST)
    mine = pl.ds(pl.multiple_of(col * piece, piece), piece)
    coret[mine, :] = mixed.astype(BF16)
    core_copies = [
        remote(coret.at[mine], coret.at[mine], core_send.at[d - 1], core_recv.at[d - 1], col=flip(d))
        for d in range(1, n_col)
    ]
    for copy in core_copies:
        copy.start()

    for h in order[1:]:
        if h != bits[0]:
            for q in range(CHUNKS):
                product(0, own, flip(h), q)
    loads["tile1"].wait()
    for q in range(CHUNKS):
        product(1, beside, col, q)
    for h in order[1:]:
        for q in range(CHUNKS):
            arrive(side_copies, h, q)
            begin(side_copies, h, q)
            product(1, beside, flip(h), q)

    loads["bout"].wait()
    for copy in core_copies:
        copy.wait_recv()
    out_ref[...] = acc[...] + jnp.dot(coret[...], bout[...], preferred_element_type=F32)

    for copy in part_copies + table_copies + core_copies:
        copy.wait_send()
    for copy in list(own_copies.values()) + list(side_copies.values()):
        copy.wait_send()
    for (_, p), copy in near_copies.items():
        pl.when(near_when[p])(copy.wait_send)


def body(
    n_cell, n_col,
    grad, near_tiles, tile_count, near_offset, far_src, far_count, far_cores, basis_out, basis_in
):
    rows, width = grad.shape
    slots, _, clus = near_tiles.shape[1:]
    far, rank = far_cores.shape[1:3]
    size, piece = rows // CHUNKS, width // n_col
    dma = lambda n: pltpu.SemaphoreType.DMA((max(n, 1),))
    hbm = pl.BlockSpec(memory_space=pltpu.HBM)
    out = pl.pallas_call(
        functools.partial(kernel, n_cell, n_col),
        out_shape=pltpu.VMEM((width, rows), F32),
        in_specs=[hbm] * 9,
        out_specs=pl.BlockSpec(memory_space=pltpu.VMEM),
        scratch_shapes=[
            pltpu.SMEM(tile_count.shape, jnp.int32),
            pltpu.SMEM(near_offset.shape, jnp.int32),
            pltpu.SMEM(far_src.shape, jnp.int32),
            pltpu.SMEM(far_count.shape, jnp.int32),
            pltpu.VMEM((width, rows), F32),
            pltpu.VMEM((slots, rows, clus), BF16),
            pltpu.VMEM((far, rank, rank), F32),
            pltpu.VMEM((rank, rows), BF16),
            pltpu.VMEM((rank, rows), BF16),
            pltpu.VMEM((n_col, CHUNKS, width, size), BF16),
            pltpu.VMEM((len(OFFSETS), CHUNKS, width, size), BF16),
            pltpu.VMEM((n_col, CHUNKS, width, size), BF16),
            pltpu.VMEM((width, rank), F32),
            pltpu.VMEM((n_col - 1, piece, rank), F32),
            pltpu.VMEM((n_cell, piece, rank), F32),
            pltpu.VMEM((rank, far * rank), F32),
            pltpu.VMEM((width, rank), BF16),
            pltpu.VMEM((width, rows), F32),
            dma(10),
            dma((n_col - 1) * CHUNKS), dma((n_col - 1) * CHUNKS),
            dma(len(OFFSETS) * CHUNKS), dma(len(OFFSETS) * CHUNKS),
            dma((n_col - 1) * CHUNKS), dma((n_col - 1) * CHUNKS),
            dma(n_col - 1), dma(n_col - 1),
            dma(n_cell - 1), dma(n_cell - 1),
            dma(n_col - 1), dma(n_col - 1),
        ],
        compiler_params=pltpu.CompilerParams(
            collective_id=0, has_side_effects=True, vmem_limit_bytes=56 * 1024 * 1024
        ),
    )(tile_count, near_offset, far_src, far_count, grad.T, near_tiles, far_cores, basis_out.T, basis_in.T)
    return out.T


def solution(mesh):
    placed = (
        P(("chain", "cell", "col"), None),
        P("cell", None, "col", None),
        P(),
        P(),
        P(),
        P(),
        P("cell", None, None, None),
        P(("cell", "col"), None),
        P(("cell", "col"), None),
    )
    return jax.shard_map(
        functools.partial(body, mesh.shape["cell"], mesh.shape["col"]),
        mesh=mesh,
        in_specs=placed,
        out_specs=P(("chain", "cell", "col"), None),
        check_vma=False,
    )
```

```python
import functools

import jax
import jax.numpy as jnp
from jax import lax
from jax.experimental import pallas as pl
from jax.experimental.pallas import tpu as pltpu
from jax.sharding import PartitionSpec as P

MESH = pl.DeviceIdType.MESH
OFFSETS = (-2, -1, 1, 2)
CHUNKS = 2
F32 = jnp.float32
BF16 = jnp.bfloat16


def remote(src, dst, send, recv, **where):
    return pltpu.make_async_remote_copy(
        src_ref=src, dst_ref=dst, send_sem=send, recv_sem=recv, device_id=where, device_id_type=MESH
    )


def across(a, b, **kw):
    return lax.dot_general(a, b, (((1,), (1,)), ((), ())), preferred_element_type=F32, **kw)


def kernel(
    n_cell, n_col,
    count_hbm, offset_hbm, fsrc_hbm, fcount_hbm, grad_hbm, tiles_hbm, cores_hbm, bout_hbm, bin_hbm,
    acc,
    count_ref, offset_ref, fsrc_ref, fcount_ref,
    grad, tiles, cores, bout, bin_,
    own, near, beside, ppt, part, table, flat, coret,
    local_sem, own_send, own_recv, near_send, near_recv, side_send, side_recv,
    part_send, part_recv, table_send, table_recv, core_send, core_recv,
):
    cell = lax.axis_index("cell")
    col = lax.axis_index("col")
    width, rows = grad.shape
    size = rows // CHUNKS
    piece = width // n_col
    bits = [1 << b for b in reversed(range(n_col.bit_length() - 1))]

    def flip(d):
        value = col
        for b in bits:
            if d & b:
                value = value + b - 2 * b * lax.rem(value // b, 2)
        return value

    barrier = pltpu.get_barrier_semaphore()
    for d in range(1, n_col):
        pl.semaphore_signal(barrier, inc=1, device_id={"col": flip(d)}, device_id_type=MESH)
    for d in range(1, n_cell):
        pl.semaphore_signal(
            barrier, inc=1, device_id={"cell": lax.rem(cell + d, n_cell)}, device_id_type=MESH
        )

    pairs = {
        "grad": (grad_hbm, grad), "bin": (bin_hbm, bin_),
        "count": (count_hbm, count_ref), "offset": (offset_hbm, offset_ref),
        "fsrc": (fsrc_hbm, fsrc_ref), "fcount": (fcount_hbm, fcount_ref),
        "cores": (cores_hbm.at[0], cores), "tile0": (tiles_hbm.at[0, 0], tiles.at[0]),
        "bout": (bout_hbm, bout), "tile1": (tiles_hbm.at[0, 1], tiles.at[1]),
    }
    loads = {
        name: pltpu.make_async_copy(src, dst, local_sem.at[i])
        for i, (name, (src, dst)) in enumerate(pairs.items())
    }
    for name in ("grad", "bin", "count", "offset"):
        loads[name].start()

    for p, step in enumerate(OFFSETS):
        @pl.when((cell + step < 0) | (cell + step >= n_cell))
        def _():
            near[p] = jnp.zeros(near.shape[1:], BF16)
    loads["grad"].wait()
    rounded = grad[...].astype(BF16)
    for q in range(CHUNKS):
        own[col, q] = rounded[:, q * size:(q + 1) * size]

    up, down = jnp.minimum(cell + 1, n_cell - 1), jnp.maximum(cell - 1, 0)
    below, above = cell > 0, cell < n_cell - 1
    inner = below & above
    near_copies, near_when = {}, {}
    for q in range(CHUNKS):
        for p, src, target, when in (
            (0, near.at[1, q], up, inner), (1, own.at[col, q], up, above),
            (2, own.at[col, q], down, below), (3, near.at[2, q], down, inner),
        ):
            index = q * len(OFFSETS) + p
            near_copies[q, p] = remote(
                src, near.at[p, q], near_send.at[index], near_recv.at[index], cell=target)
            near_when[p] = when

    def near_start(q, p):
        pl.when(near_when[p])(near_copies[q, p].start)

    def near_arrive(q, p):
        step = OFFSETS[p]
        pl.when((cell + step >= 0) & (cell + step < n_cell))(near_copies[q, p].wait_recv)

    def cube(buf, send, recv):
        copies, index, held = {}, 0, [0]
        for b in bits:
            for h in list(held):
                slot = flip(h)
                for q in range(CHUNKS):
                    copies[h, q, b] = remote(
                        buf.at[slot, q], buf.at[slot, q], send.at[index], recv.at[index], col=flip(b))
                    index += 1
            held += [h ^ b for h in held]
        return copies, held

    own_copies, order = cube(own, own_send, own_recv)
    side_copies, _ = cube(beside, side_send, side_recv)

    def begin(copies, h, q):
        for (held, chunk, b), copy in copies.items():
            if held == h and chunk == q:
                copy.start()

    def arrive(copies, h, q):
        for (held, chunk, b), copy in copies.items():
            if held ^ b == h and chunk == q:
                copy.wait_recv()

    pl.semaphore_wait(barrier, (n_col - 1) + (n_cell - 1))

    def first(q):
        near_start(q, 1)
        near_start(q, 2)
        begin(own_copies, 0, q)

    first(0)
    loads["bin"].wait()
    ppt[...] = across(rounded, bin_[...])
    part_copies = [
        remote(ppt.at[pl.ds(pl.multiple_of(flip(d) * piece, piece), piece)], part.at[d - 1],
               part_send.at[d - 1], part_recv.at[d - 1], col=flip(d))
        for d in range(1, n_col)
    ]
    for copy in part_copies:
        copy.start()

    for q in range(1, CHUNKS):
        first(q)
    for name in ("tile0", "cores", "fsrc", "fcount", "tile1", "bout"):
        loads[name].start()

    def product(tile, buf, slot, chunks=range(CHUNKS)):
        total = acc[...]
        for q in chunks:
            columns = pl.ds(pl.multiple_of(slot * rows + q * size, size), size)
            total = total + across(tiles[tile, :, columns], buf[slot, q])
        acc[...] = total

    acc[...] = jnp.zeros_like(acc)
    for copy in part_copies:
        copy.wait_recv()
    total = ppt[pl.ds(pl.multiple_of(col * piece, piece), piece), :]
    for d in range(1, n_col):
        total = total + part[d - 1]
    table[cell] = total
    table_copies = [
        remote(table.at[cell], table.at[cell], table_send.at[d - 1], table_recv.at[d - 1],
               cell=lax.rem(cell + d, n_cell))
        for d in range(1, n_cell)
    ]
    for copy in table_copies:
        copy.start()

    for q in range(CHUNKS):
        near_arrive(q, 1)
        near_start(q, 0)
        near_arrive(q, 2)
        near_start(q, 3)
    loads["tile0"].wait()
    product(0, own, col)
    for h in order[1:]:
        for q in range(CHUNKS):
            arrive(own_copies, h, q)
            begin(own_copies, h, q)
        if h == bits[0]:
            product(0, own, flip(h))

    for name in ("cores", "fsrc", "fcount", "count", "offset"):
        loads[name].wait()
    rank = cores.shape[1]
    for k in range(0, cores.shape[0], 2):
        flat[:, k * rank:(k + 2) * rank] = jnp.concatenate([cores[k], cores[k + 1]], axis=1)

    offset = offset_ref[cell]
    use = count_ref[cell] == 2
    for q in range(CHUNKS):
        near_arrive(q, 0)
        near_arrive(q, 3)
        picked = jnp.zeros(near.shape[2:], BF16)
        for p, step in enumerate(OFFSETS):
            picked = jnp.where(use & (offset == step), near[p, q], picked)
        beside[col, q] = picked
        begin(side_copies, 0, q)

    for copy in table_copies:
        copy.wait_recv()
    used = fcount_ref[cell]
    picks = []
    for k in range(cores.shape[0]):
        source = table[fsrc_ref[cell, k]]
        picks.append(jnp.where(k < used, source, jnp.zeros_like(source)))
    mixed = across(jnp.concatenate(picks, axis=1), flat[...], precision=lax.Precision.HIGHEST)
    mine = pl.ds(pl.multiple_of(col * piece, piece), piece)
    coret[mine, :] = mixed.astype(BF16)
    core_copies = [
        remote(coret.at[mine], coret.at[mine], core_send.at[d - 1], core_recv.at[d - 1], col=flip(d))
        for d in range(1, n_col)
    ]
    for copy in core_copies:
        copy.start()

    for h in order[1:]:
        if h != bits[0]:
            product(0, own, flip(h))
    loads["tile1"].wait()
    product(1, beside, col)
    loads["bout"].wait()
    flipped = bout[...].T
    for h in order[1:]:
        for q in range(CHUNKS):
            arrive(side_copies, h, q)
            begin(side_copies, h, q)
        if h != order[-1]:
            product(1, beside, flip(h))
        if h == order[-2]:
            for copy in core_copies:
                copy.wait_recv()
            acc[...] += across(flipped, coret[...])
    product(1, beside, flip(order[-1]))

    for copy in part_copies + table_copies + core_copies:
        copy.wait_send()
    for copy in list(own_copies.values()) + list(side_copies.values()):
        copy.wait_send()
    for (_, p), copy in near_copies.items():
        pl.when(near_when[p])(copy.wait_send)


def body(
    n_cell, n_col,
    grad, near_tiles, tile_count, near_offset, far_src, far_count, far_cores, basis_out, basis_in
):
    rows, width = grad.shape
    slots, _, clus = near_tiles.shape[1:]
    far, rank = far_cores.shape[1:3]
    size, piece = rows // CHUNKS, width // n_col
    dma = lambda n: pltpu.SemaphoreType.DMA((max(n, 1),))
    hbm = pl.BlockSpec(memory_space=pltpu.HBM)
    return pl.pallas_call(
        functools.partial(kernel, n_cell, n_col),
        out_shape=pltpu.VMEM((rows, width), F32),
        in_specs=[hbm] * 9,
        out_specs=pl.BlockSpec(memory_space=pltpu.VMEM),
        scratch_shapes=[
            pltpu.SMEM(tile_count.shape, jnp.int32),
            pltpu.SMEM(near_offset.shape, jnp.int32),
            pltpu.SMEM(far_src.shape, jnp.int32),
            pltpu.SMEM(far_count.shape, jnp.int32),
            pltpu.VMEM((width, rows), F32),
            pltpu.VMEM((slots, rows, clus), BF16),
            pltpu.VMEM((far, rank, rank), F32),
            pltpu.VMEM((rank, rows), BF16),
            pltpu.VMEM((rank, rows), BF16),
            pltpu.VMEM((n_col, CHUNKS, width, size), BF16),
            pltpu.VMEM((len(OFFSETS), CHUNKS, width, size), BF16),
            pltpu.VMEM((n_col, CHUNKS, width, size), BF16),
            pltpu.VMEM((width, rank), F32),
            pltpu.VMEM((n_col - 1, piece, rank), F32),
            pltpu.VMEM((n_cell, piece, rank), F32),
            pltpu.VMEM((rank, far * rank), F32),
            pltpu.VMEM((width, rank), BF16),
            dma(10),
            dma((n_col - 1) * CHUNKS), dma((n_col - 1) * CHUNKS),
            dma(len(OFFSETS) * CHUNKS), dma(len(OFFSETS) * CHUNKS),
            dma((n_col - 1) * CHUNKS), dma((n_col - 1) * CHUNKS),
            dma(n_col - 1), dma(n_col - 1),
            dma(n_cell - 1), dma(n_cell - 1),
            dma(n_col - 1), dma(n_col - 1),
        ],
        compiler_params=pltpu.CompilerParams(
            collective_id=0, has_side_effects=True, vmem_limit_bytes=56 * 1024 * 1024
        ),
    )(tile_count, near_offset, far_src, far_count, grad.T, near_tiles, far_cores, basis_out.T, basis_in.T)


def solution(mesh):
    placed = (
        P(("chain", "cell", "col"), None),
        P("cell", None, "col", None),
        P(),
        P(),
        P(),
        P(),
        P("cell", None, None, None),
        P(("cell", "col"), None),
        P(("cell", "col"), None),
    )
    return jax.shard_map(
        functools.partial(body, mesh.shape["cell"], mesh.shape["col"]),
        mesh=mesh,
        in_specs=placed,
        out_specs=P(("chain", "cell", "col"), None),
        check_vma=False,
    )
```

```python
import functools

import jax
import jax.numpy as jnp
from jax import lax
from jax.experimental import pallas as pl
from jax.experimental.pallas import tpu as pltpu
from jax.sharding import PartitionSpec as P

MESH = pl.DeviceIdType.MESH
OFFSETS = (-2, -1, 1, 2)
CHUNKS = 2
F32 = jnp.float32
BF16 = jnp.bfloat16


def remote(src, dst, send, recv, **where):
    return pltpu.make_async_remote_copy(
        src_ref=src, dst_ref=dst, send_sem=send, recv_sem=recv, device_id=where, device_id_type=MESH
    )


def across(a, b, **kw):
    return lax.dot_general(a, b, (((1,), (1,)), ((), ())), preferred_element_type=F32, **kw)


def kernel(
    n_cell, n_col,
    count_hbm, offset_hbm, fsrc_hbm, fcount_hbm, grad_hbm, tiles_hbm, cores_hbm, bout_hbm, bin_hbm,
    acc,
    count_ref, offset_ref, fsrc_ref, fcount_ref,
    grad, tiles, cores, bout, bin_,
    own, near, beside, ppt, part, table, flat, coret,
    local_sem, own_send, own_recv, near_send, near_recv, side_send, side_recv,
    part_send, part_recv, table_send, table_recv, core_send, core_recv,
):
    cell = lax.axis_index("cell")
    col = lax.axis_index("col")
    width, rows = grad.shape
    size = rows // CHUNKS
    piece = width // n_col
    bits = [1 << b for b in reversed(range(n_col.bit_length() - 1))]

    def flip(d):
        value = col
        for b in bits:
            if d & b:
                value = value + b - 2 * b * lax.rem(value // b, 2)
        return value

    barrier = pltpu.get_barrier_semaphore()
    for d in range(1, n_col):
        pl.semaphore_signal(barrier, inc=1, device_id={"col": flip(d)}, device_id_type=MESH)
    for d in range(1, n_cell):
        pl.semaphore_signal(
            barrier, inc=1, device_id={"cell": lax.rem(cell + d, n_cell)}, device_id_type=MESH
        )

    pairs = {
        "grad": (grad_hbm, grad), "bin": (bin_hbm, bin_),
        "count": (count_hbm, count_ref), "offset": (offset_hbm, offset_ref),
        "fsrc": (fsrc_hbm, fsrc_ref), "fcount": (fcount_hbm, fcount_ref),
        "cores": (cores_hbm.at[0], cores), "tile0": (tiles_hbm.at[0, 0], tiles.at[0]),
        "bout": (bout_hbm, bout), "tile1": (tiles_hbm.at[0, 1], tiles.at[1]),
    }
    loads = {
        name: pltpu.make_async_copy(src, dst, local_sem.at[i])
        for i, (name, (src, dst)) in enumerate(pairs.items())
    }
    for name in ("grad", "bin", "count", "offset"):
        loads[name].start()

    for p, step in enumerate(OFFSETS):
        @pl.when((cell + step < 0) | (cell + step >= n_cell))
        def _():
            near[p] = jnp.zeros(near.shape[1:], BF16)
    loads["grad"].wait()
    rounded = grad[...].astype(BF16)
    for q in range(CHUNKS):
        own[col, q] = rounded[:, q * size:(q + 1) * size]

    near_copies, near_when = {}, {}
    for q in range(CHUNKS):
        for p, step in enumerate(OFFSETS):
            index = q * len(OFFSETS) + p
            near_copies[q, p] = remote(
                own.at[col, q], near.at[p, q], near_send.at[index], near_recv.at[index],
                cell=jnp.clip(cell - step, 0, n_cell - 1))
            near_when[p] = (cell - step >= 0) & (cell - step < n_cell)

    def near_start(q, p):
        pl.when(near_when[p])(near_copies[q, p].start)

    def near_arrive(q, p):
        step = OFFSETS[p]
        pl.when((cell + step >= 0) & (cell + step < n_cell))(near_copies[q, p].wait_recv)

    order = list(range(2, n_col)) + [1]

    def spread(buf, send, recv):
        return {
            (d, q): remote(
                buf.at[col, q], buf.at[col, q], send.at[(d - 1) * CHUNKS + q],
                recv.at[(d - 1) * CHUNKS + q], col=flip(d))
            for d in range(1, n_col) for q in range(CHUNKS)
        }

    own_copies = spread(own, own_send, own_recv)
    side_copies = spread(beside, side_send, side_recv)
    part_copies = [
        remote(ppt.at[pl.ds(pl.multiple_of(flip(d) * piece, piece), piece)], part.at[d - 1],
               part_send.at[d - 1], part_recv.at[d - 1], col=flip(d))
        for d in range(1, n_col)
    ]
    table_copies = [
        remote(table.at[cell], table.at[cell], table_send.at[d - 1], table_recv.at[d - 1],
               cell=lax.rem(cell + d, n_cell))
        for d in range(1, n_cell)
    ]

    loads["bin"].wait()
    ppt[...] = across(rounded, bin_[...])
    pl.semaphore_wait(barrier, (n_col - 1) + (n_cell - 1))

    for copy in part_copies:
        copy.start()
    for p in (0, 3, 1, 2):
        near_start(0, p)
    for q in range(CHUNKS):
        for d in order:
            own_copies[d, q].start()
    for name in ("tile0", "cores", "fsrc", "fcount", "tile1", "bout"):
        loads[name].start()

    for copy in part_copies:
        copy.wait_recv()
    total = ppt[pl.ds(pl.multiple_of(col * piece, piece), piece), :]
    for d in range(1, n_col):
        total = total + part[d - 1]
    table[cell] = total
    for copy in table_copies:
        copy.start()
    for q in range(1, CHUNKS):
        for p in (0, 3, 1, 2):
            near_start(q, p)

    def product(tile, buf, slot, q):
        columns = pl.ds(pl.multiple_of(slot * rows + q * size, size), size)
        acc[...] += across(buf[slot, q], tiles[tile, :, columns])

    def pick(q):
        picked = jnp.zeros(near.shape[2:], BF16)
        for p, step in enumerate(OFFSETS):
            near_arrive(q, p)
            picked = jnp.where(use & (offset == step), near[p, q], picked)
        beside[col, q] = picked
        for d in order:
            side_copies[d, q].start()

    acc[...] = jnp.zeros_like(acc)
    for name in ("count", "offset"):
        loads[name].wait()
    offset = offset_ref[cell]
    use = count_ref[cell] == 2
    loads["tile0"].wait()
    for q in range(CHUNKS):
        product(0, own, col, q)
    for name in ("cores", "fsrc", "fcount"):
        loads[name].wait()
    rank = cores.shape[1]
    for k in range(0, cores.shape[0], 2):
        flat[:, k * rank:(k + 2) * rank] = jnp.concatenate([cores[k], cores[k + 1]], axis=1)
    pick(0)
    for q in range(CHUNKS):
        for d in reversed(order):
            own_copies[d, q].wait_recv()
            if q == 0:
                product(0, own, flip(d), q)
    for q in range(1, CHUNKS):
        pick(q)

    for copy in table_copies:
        copy.wait_recv()
    used = fcount_ref[cell]
    picks = []
    for k in range(cores.shape[0]):
        source = table[fsrc_ref[cell, k]]
        picks.append(jnp.where(k < used, source, jnp.zeros_like(source)))
    mixed = across(jnp.concatenate(picks, axis=1), flat[...], precision=lax.Precision.HIGHEST)
    mine = pl.ds(pl.multiple_of(col * piece, piece), piece)
    coret[mine, :] = mixed.astype(BF16)
    core_copies = [
        remote(coret.at[mine], coret.at[mine], core_send.at[d - 1], core_recv.at[d - 1], col=flip(d))
        for d in range(1, n_col)
    ]
    for copy in core_copies:
        copy.start()

    for q in range(1, CHUNKS):
        for d in order:
            product(0, own, flip(d), q)
    loads["tile1"].wait()
    for q in range(CHUNKS):
        product(1, beside, col, q)
    for q in range(CHUNKS):
        if q == CHUNKS - 1:
            loads["bout"].wait()
            for copy in core_copies:
                copy.wait_recv()
            acc[...] += jnp.dot(coret[...], bout[...], preferred_element_type=F32)
        for d in reversed(order):
            side_copies[d, q].wait_recv()
            product(1, beside, flip(d), q)

    for copy in part_copies + table_copies + core_copies:
        copy.wait_send()
    for copy in list(own_copies.values()) + list(side_copies.values()):
        copy.wait_send()
    for (_, p), copy in near_copies.items():
        pl.when(near_when[p])(copy.wait_send)


def body(
    n_cell, n_col,
    grad, near_tiles, tile_count, near_offset, far_src, far_count, far_cores, basis_out, basis_in
):
    rows, width = grad.shape
    slots, _, clus = near_tiles.shape[1:]
    far, rank = far_cores.shape[1:3]
    size, piece = rows // CHUNKS, width // n_col
    dma = lambda n: pltpu.SemaphoreType.DMA((max(n, 1),))
    hbm = pl.BlockSpec(memory_space=pltpu.HBM)
    out = pl.pallas_call(
        functools.partial(kernel, n_cell, n_col),
        out_shape=pltpu.VMEM((width, rows), F32),
        in_specs=[hbm] * 9,
        out_specs=pl.BlockSpec(memory_space=pltpu.VMEM),
        scratch_shapes=[
            pltpu.SMEM(tile_count.shape, jnp.int32),
            pltpu.SMEM(near_offset.shape, jnp.int32),
            pltpu.SMEM(far_src.shape, jnp.int32),
            pltpu.SMEM(far_count.shape, jnp.int32),
            pltpu.VMEM((width, rows), F32),
            pltpu.VMEM((slots, rows, clus), BF16),
            pltpu.VMEM((far, rank, rank), F32),
            pltpu.VMEM((rank, rows), BF16),
            pltpu.VMEM((rank, rows), BF16),
            pltpu.VMEM((n_col, CHUNKS, width, size), BF16),
            pltpu.VMEM((len(OFFSETS), CHUNKS, width, size), BF16),
            pltpu.VMEM((n_col, CHUNKS, width, size), BF16),
            pltpu.VMEM((width, rank), F32),
            pltpu.VMEM((n_col - 1, piece, rank), F32),
            pltpu.VMEM((n_cell, piece, rank), F32),
            pltpu.VMEM((rank, far * rank), F32),
            pltpu.VMEM((width, rank), BF16),
            dma(10),
            dma((n_col - 1) * CHUNKS), dma((n_col - 1) * CHUNKS),
            dma(len(OFFSETS) * CHUNKS), dma(len(OFFSETS) * CHUNKS),
            dma((n_col - 1) * CHUNKS), dma((n_col - 1) * CHUNKS),
            dma(n_col - 1), dma(n_col - 1),
            dma(n_cell - 1), dma(n_cell - 1),
            dma(n_col - 1), dma(n_col - 1),
        ],
        compiler_params=pltpu.CompilerParams(
            collective_id=0, has_side_effects=True, vmem_limit_bytes=56 * 1024 * 1024
        ),
    )(tile_count, near_offset, far_src, far_count, grad.T, near_tiles, far_cores, basis_out.T, basis_in.T)
    return out.T


def solution(mesh):
    placed = (
        P(("chain", "cell", "col"), None),
        P("cell", None, "col", None),
        P(),
        P(),
        P(),
        P(),
        P("cell", None, None, None),
        P(("cell", "col"), None),
        P(("cell", "col"), None),
    )
    return jax.shard_map(
        functools.partial(body, mesh.shape["cell"], mesh.shape["col"]),
        mesh=mesh,
        in_specs=placed,
        out_specs=P(("chain", "cell", "col"), None),
        check_vma=False,
    )
```

```python
import functools

import jax
import jax.numpy as jnp
from jax import lax
from jax.experimental import pallas as pl
from jax.experimental.pallas import tpu as pltpu
from jax.sharding import PartitionSpec as P

MESH = pl.DeviceIdType.MESH
OFFSETS = (-2, -1, 1, 2)
CHUNKS = 2
F32 = jnp.float32
BF16 = jnp.bfloat16


def remote(src, dst, send, recv, **where):
    return pltpu.make_async_remote_copy(
        src_ref=src, dst_ref=dst, send_sem=send, recv_sem=recv, device_id=where, device_id_type=MESH
    )


def across(a, b, **kw):
    return lax.dot_general(a, b, (((1,), (1,)), ((), ())), preferred_element_type=F32, **kw)


def kernel(
    n_cell, n_col,
    count_hbm, offset_hbm, fsrc_hbm, fcount_hbm, grad_hbm, tiles_hbm, cores_hbm, bout_hbm, bin_hbm,
    acc,
    count_ref, offset_ref, fsrc_ref, fcount_ref,
    grad, tiles, cores, bout, bin_,
    own, near, beside, ppt, part, table, flat, coret,
    local_sem, own_send, own_recv, near_send, near_recv, side_send, side_recv,
    part_send, part_recv, table_send, table_recv, core_send, core_recv,
):
    cell = lax.axis_index("cell")
    col = lax.axis_index("col")
    width, rows = grad.shape
    size = rows // CHUNKS
    piece = width // n_col
    bits = [1 << b for b in reversed(range(n_col.bit_length() - 1))]

    def flip(d):
        value = col
        for b in bits:
            if d & b:
                value = value + b - 2 * b * lax.rem(value // b, 2)
        return value

    barrier = pltpu.get_barrier_semaphore()
    for d in range(1, n_col):
        pl.semaphore_signal(barrier, inc=1, device_id={"col": flip(d)}, device_id_type=MESH)
    for d in range(1, n_cell):
        pl.semaphore_signal(
            barrier, inc=1, device_id={"cell": lax.rem(cell + d, n_cell)}, device_id_type=MESH
        )

    pairs = {
        "grad": (grad_hbm, grad), "bin": (bin_hbm, bin_),
        "count": (count_hbm, count_ref), "offset": (offset_hbm, offset_ref),
        "fsrc": (fsrc_hbm, fsrc_ref), "fcount": (fcount_hbm, fcount_ref),
        "cores": (cores_hbm.at[0], cores), "tile0": (tiles_hbm.at[0, 0], tiles.at[0]),
        "bout": (bout_hbm, bout), "tile1": (tiles_hbm.at[0, 1], tiles.at[1]),
    }
    loads = {
        name: pltpu.make_async_copy(src, dst, local_sem.at[i])
        for i, (name, (src, dst)) in enumerate(pairs.items())
    }
    for name in ("grad", "bin", "count", "offset"):
        loads[name].start()

    for p, step in enumerate(OFFSETS):
        @pl.when((cell + step < 0) | (cell + step >= n_cell))
        def _():
            near[p] = jnp.zeros(near.shape[1:], BF16)
    loads["grad"].wait()
    rounded = grad[...].astype(BF16)
    for q in range(CHUNKS):
        own[col, q] = rounded[:, q * size:(q + 1) * size]

    near_copies, near_when = {}, {}
    for q in range(CHUNKS):
        for p, step in enumerate(OFFSETS):
            index = q * len(OFFSETS) + p
            near_copies[q, p] = remote(
                own.at[col, q], near.at[p, q], near_send.at[index], near_recv.at[index],
                cell=jnp.clip(cell - step, 0, n_cell - 1))
            near_when[p] = (cell - step >= 0) & (cell - step < n_cell)

    def near_start(q, p):
        pl.when(near_when[p])(near_copies[q, p].start)

    def near_arrive(q, p):
        step = OFFSETS[p]
        pl.when((cell + step >= 0) & (cell + step < n_cell))(near_copies[q, p].wait_recv)

    order = list(range(2, n_col)) + [1]

    def spread(buf, send, recv):
        return {
            (d, q): remote(
                buf.at[col, q], buf.at[col, q], send.at[(d - 1) * CHUNKS + q],
                recv.at[(d - 1) * CHUNKS + q], col=flip(d))
            for d in range(1, n_col) for q in range(CHUNKS)
        }

    own_copies = spread(own, own_send, own_recv)
    side_copies = spread(beside, side_send, side_recv)
    part_copies = [
        remote(ppt.at[pl.ds(pl.multiple_of(flip(d) * piece, piece), piece)], part.at[d - 1],
               part_send.at[d - 1], part_recv.at[d - 1], col=flip(d))
        for d in range(1, n_col)
    ]
    table_copies = [
        remote(table.at[cell], table.at[cell], table_send.at[d - 1], table_recv.at[d - 1],
               cell=lax.rem(cell + d, n_cell))
        for d in range(1, n_cell)
    ]

    loads["bin"].wait()
    ppt[...] = across(rounded, bin_[...])
    pl.semaphore_wait(barrier, (n_col - 1) + (n_cell - 1))

    for copy in part_copies:
        copy.start()
    for p in (0, 3, 1, 2):
        near_start(0, p)
    for q in range(CHUNKS):
        for d in order:
            own_copies[d, q].start()
    for name in ("tile0", "cores", "fsrc", "fcount", "tile1", "bout"):
        loads[name].start()

    for copy in part_copies:
        copy.wait_recv()
    total = ppt[pl.ds(pl.multiple_of(col * piece, piece), piece), :]
    for d in range(1, n_col):
        total = total + part[d - 1]
    table[cell] = total
    for copy in table_copies:
        copy.start()
    for q in range(1, CHUNKS):
        for p in (0, 3, 1, 2):
            near_start(q, p)

    def product(tile, buf, chunks):
        places = [(j, q) for j in range(n_col) for q in chunks]
        blocks = jnp.concatenate([buf[j, q] for j, q in places], axis=1)
        columns = jnp.concatenate(
            [tiles[tile, :, j * rows + q * size:j * rows + (q + 1) * size] for j, q in places], axis=1)
        return across(blocks, columns)

    def pick(q):
        picked = jnp.zeros(near.shape[2:], BF16)
        for p, step in enumerate(OFFSETS):
            near_arrive(q, p)
            picked = jnp.where(use & (offset == step), near[p, q], picked)
        beside[col, q] = picked
        for d in order:
            side_copies[d, q].start()

    for name in ("count", "offset", "cores", "fsrc", "fcount"):
        loads[name].wait()
    offset = offset_ref[cell]
    use = count_ref[cell] == 2
    rank = cores.shape[1]
    for k in range(0, cores.shape[0], 2):
        flat[:, k * rank:(k + 2) * rank] = jnp.concatenate([cores[k], cores[k + 1]], axis=1)
    pick(0)
    loads["tile0"].wait()
    for copy in own_copies.values():
        copy.wait_recv()
    acc[...] = product(0, own, range(CHUNKS))
    for q in range(1, CHUNKS):
        pick(q)

    for copy in table_copies:
        copy.wait_recv()
    used = fcount_ref[cell]
    picks = []
    for k in range(cores.shape[0]):
        source = table[fsrc_ref[cell, k]]
        picks.append(jnp.where(k < used, source, jnp.zeros_like(source)))
    mixed = across(jnp.concatenate(picks, axis=1), flat[...], precision=lax.Precision.HIGHEST)
    mine = pl.ds(pl.multiple_of(col * piece, piece), piece)
    coret[mine, :] = mixed.astype(BF16)
    core_copies = [
        remote(coret.at[mine], coret.at[mine], core_send.at[d - 1], core_recv.at[d - 1], col=flip(d))
        for d in range(1, n_col)
    ]
    for copy in core_copies:
        copy.start()

    loads["tile1"].wait()
    for q in range(CHUNKS):
        if q == CHUNKS - 1:
            loads["bout"].wait()
            for copy in core_copies:
                copy.wait_recv()
            acc[...] += jnp.dot(coret[...], bout[...], preferred_element_type=F32)
        for d in order:
            side_copies[d, q].wait_recv()
        acc[...] += product(1, beside, [q])

    for copy in part_copies + table_copies + core_copies:
        copy.wait_send()
    for copy in list(own_copies.values()) + list(side_copies.values()):
        copy.wait_send()
    for (_, p), copy in near_copies.items():
        pl.when(near_when[p])(copy.wait_send)


def body(
    n_cell, n_col,
    grad, near_tiles, tile_count, near_offset, far_src, far_count, far_cores, basis_out, basis_in
):
    rows, width = grad.shape
    slots, _, clus = near_tiles.shape[1:]
    far, rank = far_cores.shape[1:3]
    size, piece = rows // CHUNKS, width // n_col
    dma = lambda n: pltpu.SemaphoreType.DMA((max(n, 1),))
    hbm = pl.BlockSpec(memory_space=pltpu.HBM)
    out = pl.pallas_call(
        functools.partial(kernel, n_cell, n_col),
        out_shape=pltpu.VMEM((width, rows), F32),
        in_specs=[hbm] * 9,
        out_specs=pl.BlockSpec(memory_space=pltpu.VMEM),
        scratch_shapes=[
            pltpu.SMEM(tile_count.shape, jnp.int32),
            pltpu.SMEM(near_offset.shape, jnp.int32),
            pltpu.SMEM(far_src.shape, jnp.int32),
            pltpu.SMEM(far_count.shape, jnp.int32),
            pltpu.VMEM((width, rows), F32),
            pltpu.VMEM((slots, rows, clus), BF16),
            pltpu.VMEM((far, rank, rank), F32),
            pltpu.VMEM((rank, rows), BF16),
            pltpu.VMEM((rank, rows), BF16),
            pltpu.VMEM((n_col, CHUNKS, width, size), BF16),
            pltpu.VMEM((len(OFFSETS), CHUNKS, width, size), BF16),
            pltpu.VMEM((n_col, CHUNKS, width, size), BF16),
            pltpu.VMEM((width, rank), F32),
            pltpu.VMEM((n_col - 1, piece, rank), F32),
            pltpu.VMEM((n_cell, piece, rank), F32),
            pltpu.VMEM((rank, far * rank), F32),
            pltpu.VMEM((width, rank), BF16),
            dma(10),
            dma((n_col - 1) * CHUNKS), dma((n_col - 1) * CHUNKS),
            dma(len(OFFSETS) * CHUNKS), dma(len(OFFSETS) * CHUNKS),
            dma((n_col - 1) * CHUNKS), dma((n_col - 1) * CHUNKS),
            dma(n_col - 1), dma(n_col - 1),
            dma(n_cell - 1), dma(n_cell - 1),
            dma(n_col - 1), dma(n_col - 1),
        ],
        compiler_params=pltpu.CompilerParams(
            collective_id=0, has_side_effects=True, vmem_limit_bytes=56 * 1024 * 1024
        ),
    )(tile_count, near_offset, far_src, far_count, grad.T, near_tiles, far_cores, basis_out.T, basis_in.T)
    return out.T


def solution(mesh):
    placed = (
        P(("chain", "cell", "col"), None),
        P("cell", None, "col", None),
        P(),
        P(),
        P(),
        P(),
        P("cell", None, None, None),
        P(("cell", "col"), None),
        P(("cell", "col"), None),
    )
    return jax.shard_map(
        functools.partial(body, mesh.shape["cell"], mesh.shape["col"]),
        mesh=mesh,
        in_specs=placed,
        out_specs=P(("chain", "cell", "col"), None),
        check_vma=False,
    )
```

```python
import functools

import jax
import jax.numpy as jnp
from jax import lax
from jax.experimental import pallas as pl
from jax.experimental.pallas import tpu as pltpu
from jax.sharding import PartitionSpec as P

MESH = pl.DeviceIdType.MESH
OFFSETS = (-2, -1, 1, 2)
CHUNKS = 2
F32 = jnp.float32
BF16 = jnp.bfloat16


def remote(src, dst, send, recv, **where):
    return pltpu.make_async_remote_copy(
        src_ref=src, dst_ref=dst, send_sem=send, recv_sem=recv, device_id=where, device_id_type=MESH
    )


def across(a, b, **kw):
    return lax.dot_general(a, b, (((1,), (1,)), ((), ())), preferred_element_type=F32, **kw)


def kernel(
    n_cell, n_col,
    count_hbm, offset_hbm, fsrc_hbm, fcount_hbm, grad_hbm, tiles_hbm, cores_hbm, bout_hbm, bin_hbm,
    acc,
    count_ref, offset_ref, fsrc_ref, fcount_ref,
    grad, tiles, cores, bout, bin_,
    own, near, beside, ppt, part, table, flat,
    local_sem, own_send, own_recv, near_send, near_recv, side_send, side_recv,
    part_send, part_recv, table_send, table_recv,
):
    cell = lax.axis_index("cell")
    col = lax.axis_index("col")
    width, rows = grad.shape
    size = rows // CHUNKS
    bits = [1 << b for b in reversed(range(n_col.bit_length() - 1))]

    def flip(d):
        value = col
        for b in bits:
            if d & b:
                value = value + b - 2 * b * lax.rem(value // b, 2)
        return value

    barrier = pltpu.get_barrier_semaphore()
    for d in range(1, n_col):
        pl.semaphore_signal(barrier, inc=1, device_id={"col": flip(d)}, device_id_type=MESH)
    for d in range(1, n_cell):
        pl.semaphore_signal(
            barrier, inc=1, device_id={"cell": lax.rem(cell + d, n_cell)}, device_id_type=MESH
        )

    pairs = {
        "grad": (grad_hbm, grad), "bin": (bin_hbm, bin_),
        "count": (count_hbm, count_ref), "offset": (offset_hbm, offset_ref),
        "fsrc": (fsrc_hbm, fsrc_ref), "fcount": (fcount_hbm, fcount_ref),
        "cores": (cores_hbm.at[0], cores), "tile0": (tiles_hbm.at[0, 0], tiles.at[0]),
        "bout": (bout_hbm, bout), "tile1": (tiles_hbm.at[0, 1], tiles.at[1]),
    }
    loads = {
        name: pltpu.make_async_copy(src, dst, local_sem.at[i])
        for i, (name, (src, dst)) in enumerate(pairs.items())
    }
    for name in ("grad", "bin", "count", "offset"):
        loads[name].start()

    for p, step in enumerate(OFFSETS):
        @pl.when((cell + step < 0) | (cell + step >= n_cell))
        def _():
            near[p] = jnp.zeros(near.shape[1:], BF16)
    loads["grad"].wait()
    rounded = grad[...].astype(BF16)
    for q in range(CHUNKS):
        own[col, q] = rounded[:, q * size:(q + 1) * size]

    near_copies, near_when = {}, {}
    for q in range(CHUNKS):
        for p, step in enumerate(OFFSETS):
            index = q * len(OFFSETS) + p
            near_copies[q, p] = remote(
                own.at[col, q], near.at[p, q], near_send.at[index], near_recv.at[index],
                cell=jnp.clip(cell - step, 0, n_cell - 1))
            near_when[p] = (cell - step >= 0) & (cell - step < n_cell)

    def near_start(q, p):
        pl.when(near_when[p])(near_copies[q, p].start)

    def near_arrive(q, p):
        step = OFFSETS[p]
        pl.when((cell + step >= 0) & (cell + step < n_cell))(near_copies[q, p].wait_recv)

    order = list(range(2, n_col)) + [1]

    def spread(buf, send, recv):
        return {
            (d, q): remote(
                buf.at[col, q], buf.at[col, q], send.at[(d - 1) * CHUNKS + q],
                recv.at[(d - 1) * CHUNKS + q], col=flip(d))
            for d in range(1, n_col) for q in range(CHUNKS)
        }

    own_copies = spread(own, own_send, own_recv)
    side_copies = spread(beside, side_send, side_recv)
    part_copies = [
        remote(ppt, part.at[d - 1], part_send.at[d - 1], part_recv.at[d - 1], col=flip(d))
        for d in range(1, n_col)
    ]
    table_copies = [
        remote(table.at[cell], table.at[cell], table_send.at[d - 1], table_recv.at[d - 1],
               cell=lax.rem(cell + d, n_cell))
        for d in range(1, n_cell)
    ]

    pl.semaphore_wait(barrier, (n_col - 1) + (n_cell - 1))

    for p in (0, 3, 1, 2):
        near_start(0, p)
    loads["bin"].wait()
    ppt[...] = across(rounded, bin_[...])
    for copy in part_copies:
        copy.start()
    for q in range(CHUNKS):
        for d in order:
            own_copies[d, q].start()
        if q + 1 < CHUNKS:
            for p in (0, 3, 1, 2):
                near_start(q + 1, p)
    for name in ("tile0", "cores", "fsrc", "fcount", "tile1", "bout"):
        loads[name].start()

    for copy in part_copies:
        copy.wait_recv()
    total = ppt[...]
    for d in range(1, n_col):
        total = total + part[d - 1]
    table[cell] = total
    for copy in table_copies:
        copy.start()

    def product(tile, buf, chunks):
        places = [(j, q) for j in range(n_col) for q in chunks]
        blocks = jnp.concatenate([buf[j, q] for j, q in places], axis=1)
        columns = jnp.concatenate(
            [tiles[tile, :, j * rows + q * size:j * rows + (q + 1) * size] for j, q in places], axis=1)
        return across(blocks, columns)

    def pick(q):
        picked = jnp.zeros(near.shape[2:], BF16)
        for p, step in enumerate(OFFSETS):
            near_arrive(q, p)
            picked = jnp.where(use & (offset == step), near[p, q], picked)
        beside[col, q] = picked
        for d in order:
            side_copies[d, q].start()

    for name in ("count", "offset", "cores", "fsrc", "fcount"):
        loads[name].wait()
    offset = offset_ref[cell]
    use = count_ref[cell] == 2
    rank = cores.shape[1]
    for k in range(0, cores.shape[0], 2):
        flat[:, k * rank:(k + 2) * rank] = jnp.concatenate([cores[k], cores[k + 1]], axis=1)
    pick(0)
    loads["tile0"].wait()
    for copy in own_copies.values():
        copy.wait_recv()
    acc[...] = product(0, own, range(CHUNKS))
    for q in range(1, CHUNKS):
        pick(q)

    for copy in table_copies:
        copy.wait_recv()
    used = fcount_ref[cell]
    picks = []
    for k in range(cores.shape[0]):
        source = table[fsrc_ref[cell, k]]
        picks.append(jnp.where(k < used, source, jnp.zeros_like(source)))
    core = across(
        jnp.concatenate(picks, axis=1), flat[...], precision=lax.Precision.HIGHEST).astype(BF16)

    loads["tile1"].wait()
    for q in range(CHUNKS):
        if q == CHUNKS - 1:
            loads["bout"].wait()
            acc[...] += jnp.dot(core, bout[...], preferred_element_type=F32)
        for d in order:
            side_copies[d, q].wait_recv()
        acc[...] += product(1, beside, [q])

    for copy in part_copies + table_copies:
        copy.wait_send()
    for copy in list(own_copies.values()) + list(side_copies.values()):
        copy.wait_send()
    for (_, p), copy in near_copies.items():
        pl.when(near_when[p])(copy.wait_send)


def body(
    n_cell, n_col,
    grad, near_tiles, tile_count, near_offset, far_src, far_count, far_cores, basis_out, basis_in
):
    rows, width = grad.shape
    slots, _, clus = near_tiles.shape[1:]
    far, rank = far_cores.shape[1:3]
    size = rows // CHUNKS
    dma = lambda n: pltpu.SemaphoreType.DMA((max(n, 1),))
    hbm = pl.BlockSpec(memory_space=pltpu.HBM)
    out = pl.pallas_call(
        functools.partial(kernel, n_cell, n_col),
        out_shape=pltpu.VMEM((width, rows), F32),
        in_specs=[hbm] * 9,
        out_specs=pl.BlockSpec(memory_space=pltpu.VMEM),
        scratch_shapes=[
            pltpu.SMEM(tile_count.shape, jnp.int32),
            pltpu.SMEM(near_offset.shape, jnp.int32),
            pltpu.SMEM(far_src.shape, jnp.int32),
            pltpu.SMEM(far_count.shape, jnp.int32),
            pltpu.VMEM((width, rows), F32),
            pltpu.VMEM((slots, rows, clus), BF16),
            pltpu.VMEM((far, rank, rank), F32),
            pltpu.VMEM((rank, rows), BF16),
            pltpu.VMEM((rank, rows), BF16),
            pltpu.VMEM((n_col, CHUNKS, width, size), BF16),
            pltpu.VMEM((len(OFFSETS), CHUNKS, width, size), BF16),
            pltpu.VMEM((n_col, CHUNKS, width, size), BF16),
            pltpu.VMEM((width, rank), F32),
            pltpu.VMEM((n_col - 1, width, rank), F32),
            pltpu.VMEM((n_cell, width, rank), F32),
            pltpu.VMEM((rank, far * rank), F32),
            dma(10),
            dma((n_col - 1) * CHUNKS), dma((n_col - 1) * CHUNKS),
            dma(len(OFFSETS) * CHUNKS), dma(len(OFFSETS) * CHUNKS),
            dma((n_col - 1) * CHUNKS), dma((n_col - 1) * CHUNKS),
            dma(n_col - 1), dma(n_col - 1),
            dma(n_cell - 1), dma(n_cell - 1),
        ],
        compiler_params=pltpu.CompilerParams(
            collective_id=0, has_side_effects=True, vmem_limit_bytes=56 * 1024 * 1024
        ),
    )(tile_count, near_offset, far_src, far_count, grad.T, near_tiles, far_cores, basis_out.T, basis_in.T)
    return out.T


def solution(mesh):
    placed = (
        P(("chain", "cell", "col"), None),
        P("cell", None, "col", None),
        P(),
        P(),
        P(),
        P(),
        P("cell", None, None, None),
        P(("cell", "col"), None),
        P(("cell", "col"), None),
    )
    return jax.shard_map(
        functools.partial(body, mesh.shape["cell"], mesh.shape["col"]),
        mesh=mesh,
        in_specs=placed,
        out_specs=P(("chain", "cell", "col"), None),
        check_vma=False,
    )
```

```python
import functools

import jax
import jax.numpy as jnp
from jax import lax
from jax.experimental import pallas as pl
from jax.experimental.pallas import tpu as pltpu
from jax.sharding import PartitionSpec as P

MESH = pl.DeviceIdType.MESH
OFFSETS = (-2, -1, 1, 2)
CHUNKS = 4
F32 = jnp.float32
BF16 = jnp.bfloat16


def remote(src, dst, send, recv, **where):
    return pltpu.make_async_remote_copy(
        src_ref=src, dst_ref=dst, send_sem=send, recv_sem=recv, device_id=where, device_id_type=MESH
    )


def across(a, b, **kw):
    return lax.dot_general(a, b, (((1,), (1,)), ((), ())), preferred_element_type=F32, **kw)


def kernel(
    n_cell, n_col,
    count_hbm, offset_hbm, fsrc_hbm, fcount_hbm, grad_hbm, tiles_hbm, cores_hbm, bout_hbm, bin_hbm,
    acc,
    count_ref, offset_ref, fsrc_ref, fcount_ref,
    grad, tiles, cores, bout, bin_,
    own, near, beside, ppt, part, table, flat,
    local_sem, own_send, own_recv, near_send, near_recv, side_send, side_recv,
    part_send, part_recv, table_send, table_recv,
):
    cell = lax.axis_index("cell")
    col = lax.axis_index("col")
    width, rows = grad.shape
    size = rows // CHUNKS
    bits = [1 << b for b in reversed(range(n_col.bit_length() - 1))]

    def flip(d):
        value = col
        for b in bits:
            if d & b:
                value = value + b - 2 * b * lax.rem(value // b, 2)
        return value

    barrier = pltpu.get_barrier_semaphore()
    for d in range(1, n_col):
        pl.semaphore_signal(barrier, inc=1, device_id={"col": flip(d)}, device_id_type=MESH)
    for d in range(1, n_cell):
        pl.semaphore_signal(
            barrier, inc=1, device_id={"cell": lax.rem(cell + d, n_cell)}, device_id_type=MESH
        )

    pairs = {
        "grad": (grad_hbm, grad), "bin": (bin_hbm, bin_),
        "count": (count_hbm, count_ref), "offset": (offset_hbm, offset_ref),
        "fsrc": (fsrc_hbm, fsrc_ref), "fcount": (fcount_hbm, fcount_ref),
        "cores": (cores_hbm.at[0], cores), "tile0": (tiles_hbm.at[0, 0], tiles.at[0]),
        "bout": (bout_hbm, bout), "tile1": (tiles_hbm.at[0, 1], tiles.at[1]),
    }
    loads = {
        name: pltpu.make_async_copy(src, dst, local_sem.at[i])
        for i, (name, (src, dst)) in enumerate(pairs.items())
    }
    for name in ("grad", "bin", "count", "offset"):
        loads[name].start()

    for p, step in enumerate(OFFSETS):
        @pl.when((cell + step < 0) | (cell + step >= n_cell))
        def _():
            near[p] = jnp.zeros(near.shape[1:], BF16)
    loads["grad"].wait()
    rounded = grad[...].astype(BF16)
    for q in range(CHUNKS):
        own[col, q] = rounded[:, q * size:(q + 1) * size]

    near_copies, near_when = {}, {}
    for q in range(CHUNKS):
        for p, step in enumerate(OFFSETS):
            index = q * len(OFFSETS) + p
            near_copies[q, p] = remote(
                own.at[col, q], near.at[p, q], near_send.at[index], near_recv.at[index],
                cell=jnp.clip(cell - step, 0, n_cell - 1))
            near_when[p] = (cell - step >= 0) & (cell - step < n_cell)

    def near_start(q, p):
        pl.when(near_when[p])(near_copies[q, p].start)

    def near_arrive(q, p):
        step = OFFSETS[p]
        pl.when((cell + step >= 0) & (cell + step < n_cell))(near_copies[q, p].wait_recv)

    order = list(range(2, n_col)) + [1]

    def spread(buf, send, recv):
        return {
            (d, q): remote(
                buf.at[col, q], buf.at[col, q], send.at[(d - 1) * CHUNKS + q],
                recv.at[(d - 1) * CHUNKS + q], col=flip(d))
            for d in range(1, n_col) for q in range(CHUNKS)
        }

    own_copies, held = {}, [0]
    for b in bits:
        for h in held:
            slot, index = flip(h), len(own_copies)
            own_copies[h, b] = remote(
                own.at[slot], own.at[slot], own_send.at[index], own_recv.at[index], col=flip(b))
        held = held + [h ^ b for h in held]

    side_copies = spread(beside, side_send, side_recv)
    part_copies = [
        remote(ppt, part.at[d - 1], part_send.at[d - 1], part_recv.at[d - 1], col=flip(d))
        for d in range(1, n_col)
    ]
    table_copies = [
        remote(table.at[cell], table.at[cell], table_send.at[d - 1], table_recv.at[d - 1],
               cell=lax.rem(cell + d, n_cell))
        for d in range(1, n_cell)
    ]

    pl.semaphore_wait(barrier, (n_col - 1) + (n_cell - 1))

    for p in (0, 3, 1, 2):
        near_start(0, p)
    loads["bin"].wait()
    ppt[...] = across(rounded, bin_[...])
    for copy in part_copies:
        copy.start()
    for q in range(1, CHUNKS):
        for p in (0, 3, 1, 2):
            near_start(q, p)
        if q == 1:
            for b in bits:
                own_copies[0, b].start()
    for name in ("tile0", "cores", "fsrc", "fcount", "tile1", "bout"):
        loads[name].start()

    for copy in part_copies:
        copy.wait_recv()
    total = ppt[...]
    for d in range(1, n_col):
        total = total + part[d - 1]
    table[cell] = total
    for copy in table_copies:
        copy.start()

    def product(tile, buf, chunks):
        places = [(j, q) for j in range(n_col) for q in chunks]
        blocks = jnp.concatenate([buf[j, q] for j, q in places], axis=1)
        columns = jnp.concatenate(
            [tiles[tile, :, j * rows + q * size:j * rows + (q + 1) * size] for j, q in places], axis=1)
        return across(blocks, columns)

    def pick(q):
        picked = jnp.zeros(near.shape[2:], BF16)
        for p, step in enumerate(OFFSETS):
            near_arrive(q, p)
            picked = jnp.where(use & (offset == step), near[p, q], picked)
        beside[col, q] = picked
        for d in order:
            side_copies[d, q].start()

    for name in ("count", "offset", "cores", "fsrc", "fcount"):
        loads[name].wait()
    offset = offset_ref[cell]
    use = count_ref[cell] == 2
    rank = cores.shape[1]
    for k in range(0, cores.shape[0], 2):
        flat[:, k * rank:(k + 2) * rank] = jnp.concatenate([cores[k], cores[k + 1]], axis=1)
    pick(0)
    for h in held[1:]:
        for (source, b), copy in own_copies.items():
            if source ^ b == h:
                copy.wait_recv()
        for (source, b), copy in own_copies.items():
            if source == h:
                copy.start()
        if h == bits[0]:
            for q in range(1, CHUNKS):
                pick(q)
    loads["tile0"].wait()
    acc[...] = product(0, own, range(CHUNKS))

    for copy in table_copies:
        copy.wait_recv()
    used = fcount_ref[cell]
    picks = []
    for k in range(cores.shape[0]):
        source = table[fsrc_ref[cell, k]]
        picks.append(jnp.where(k < used, source, jnp.zeros_like(source)))
    core = across(
        jnp.concatenate(picks, axis=1), flat[...], precision=lax.Precision.HIGHEST).astype(BF16)

    loads["tile1"].wait()
    for d in order:
        for q in range(CHUNKS - 1):
            side_copies[d, q].wait_recv()
    acc[...] += product(1, beside, range(CHUNKS - 1))
    loads["bout"].wait()
    acc[...] += jnp.dot(core, bout[...], preferred_element_type=F32)
    for d in order:
        side_copies[d, CHUNKS - 1].wait_recv()
    acc[...] += product(1, beside, [CHUNKS - 1])

    for copy in part_copies + table_copies:
        copy.wait_send()
    for copy in list(own_copies.values()) + list(side_copies.values()):
        copy.wait_send()
    for (_, p), copy in near_copies.items():
        pl.when(near_when[p])(copy.wait_send)


def body(
    n_cell, n_col,
    grad, near_tiles, tile_count, near_offset, far_src, far_count, far_cores, basis_out, basis_in
):
    rows, width = grad.shape
    slots, _, clus = near_tiles.shape[1:]
    far, rank = far_cores.shape[1:3]
    size = rows // CHUNKS
    dma = lambda n: pltpu.SemaphoreType.DMA((max(n, 1),))
    hbm = pl.BlockSpec(memory_space=pltpu.HBM)
    out = pl.pallas_call(
        functools.partial(kernel, n_cell, n_col),
        out_shape=pltpu.VMEM((width, rows), F32),
        in_specs=[hbm] * 9,
        out_specs=pl.BlockSpec(memory_space=pltpu.VMEM),
        scratch_shapes=[
            pltpu.SMEM(tile_count.shape, jnp.int32),
            pltpu.SMEM(near_offset.shape, jnp.int32),
            pltpu.SMEM(far_src.shape, jnp.int32),
            pltpu.SMEM(far_count.shape, jnp.int32),
            pltpu.VMEM((width, rows), F32),
            pltpu.VMEM((slots, rows, clus), BF16),
            pltpu.VMEM((far, rank, rank), F32),
            pltpu.VMEM((rank, rows), BF16),
            pltpu.VMEM((rank, rows), BF16),
            pltpu.VMEM((n_col, CHUNKS, width, size), BF16),
            pltpu.VMEM((len(OFFSETS), CHUNKS, width, size), BF16),
            pltpu.VMEM((n_col, CHUNKS, width, size), BF16),
            pltpu.VMEM((width, rank), F32),
            pltpu.VMEM((n_col - 1, width, rank), F32),
            pltpu.VMEM((n_cell, width, rank), F32),
            pltpu.VMEM((rank, far * rank), F32),
            dma(10),
            dma(n_col - 1), dma(n_col - 1),
            dma(len(OFFSETS) * CHUNKS), dma(len(OFFSETS) * CHUNKS),
            dma((n_col - 1) * CHUNKS), dma((n_col - 1) * CHUNKS),
            dma(n_col - 1), dma(n_col - 1),
            dma(n_cell - 1), dma(n_cell - 1),
        ],
        compiler_params=pltpu.CompilerParams(
            collective_id=0, has_side_effects=True, vmem_limit_bytes=56 * 1024 * 1024
        ),
    )(tile_count, near_offset, far_src, far_count, grad.T, near_tiles, far_cores, basis_out.T, basis_in.T)
    return out.T


def solution(mesh):
    placed = (
        P(("chain", "cell", "col"), None),
        P("cell", None, "col", None),
        P(),
        P(),
        P(),
        P(),
        P("cell", None, None, None),
        P(("cell", "col"), None),
        P(("cell", "col"), None),
    )
    return jax.shard_map(
        functools.partial(body, mesh.shape["cell"], mesh.shape["col"]),
        mesh=mesh,
        in_specs=placed,
        out_specs=P(("chain", "cell", "col"), None),
        check_vma=False,
    )
```

```python
import functools

import jax
import jax.numpy as jnp
from jax import lax
from jax.experimental import pallas as pl
from jax.experimental.pallas import tpu as pltpu
from jax.sharding import PartitionSpec as P

MESH = pl.DeviceIdType.MESH
OFFSETS = (-2, -1, 1, 2)
CHUNKS = 4
FORWARDED = 2
F32 = jnp.float32
BF16 = jnp.bfloat16


def remote(src, dst, send, recv, **where):
    return pltpu.make_async_remote_copy(
        src_ref=src, dst_ref=dst, send_sem=send, recv_sem=recv, device_id=where, device_id_type=MESH
    )


def across(a, b, **kw):
    return lax.dot_general(a, b, (((1,), (1,)), ((), ())), preferred_element_type=F32, **kw)


def kernel(
    n_cell, n_col,
    count_hbm, offset_hbm, fsrc_hbm, fcount_hbm, grad_hbm, tiles_hbm, cores_hbm, bout_hbm, bin_hbm,
    acc,
    count_ref, offset_ref, fsrc_ref, fcount_ref,
    grad, tiles, cores, bout, bin_,
    own, near, beside, ppt, part, table, flat,
    local_sem, own_send, own_recv, near_send, near_recv, side_send, side_recv,
    part_send, part_recv, table_send, table_recv,
):
    cell = lax.axis_index("cell")
    col = lax.axis_index("col")
    width, rows = grad.shape
    size = rows // CHUNKS
    bits = [1 << b for b in reversed(range(n_col.bit_length() - 1))]

    def flip(d):
        value = col
        for b in bits:
            if d & b:
                value = value + b - 2 * b * lax.rem(value // b, 2)
        return value

    barrier = pltpu.get_barrier_semaphore()
    for d in range(1, n_col):
        pl.semaphore_signal(barrier, inc=1, device_id={"col": flip(d)}, device_id_type=MESH)
    for d in range(1, n_cell):
        pl.semaphore_signal(
            barrier, inc=1, device_id={"cell": lax.rem(cell + d, n_cell)}, device_id_type=MESH
        )

    pairs = {
        "grad": (grad_hbm, grad), "bin": (bin_hbm, bin_),
        "count": (count_hbm, count_ref), "offset": (offset_hbm, offset_ref),
        "fsrc": (fsrc_hbm, fsrc_ref), "fcount": (fcount_hbm, fcount_ref),
        "cores": (cores_hbm.at[0], cores), "tile0": (tiles_hbm.at[0, 0], tiles.at[0]),
        "bout": (bout_hbm, bout), "tile1": (tiles_hbm.at[0, 1], tiles.at[1]),
    }
    loads = {
        name: pltpu.make_async_copy(src, dst, local_sem.at[i])
        for i, (name, (src, dst)) in enumerate(pairs.items())
    }
    for name in ("grad", "bin", "count", "offset"):
        loads[name].start()

    for p, step in enumerate(OFFSETS):
        @pl.when((cell + step < 0) | (cell + step >= n_cell))
        def _():
            near[p] = jnp.zeros(near.shape[1:], BF16)
    loads["grad"].wait()
    rounded = grad[...].astype(BF16)
    for q in range(CHUNKS):
        own[col, q] = rounded[:, q * size:(q + 1) * size]

    up, down = jnp.minimum(cell + 1, n_cell - 1), jnp.maximum(cell - 1, 0)
    below, above = cell > 0, cell < n_cell - 1
    inner = below & above
    near_copies, near_when = {}, {}
    for q in range(CHUNKS):
        for p, src, target, when in (
            (0, near.at[1, q], up, inner), (1, own.at[col, q], up, above),
            (2, own.at[col, q], down, below), (3, near.at[2, q], down, inner),
        ):
            index = q * len(OFFSETS) + p
            near_copies[q, p] = remote(
                src, near.at[p, q], near_send.at[index], near_recv.at[index], cell=target)
            near_when[p] = when

    def near_start(q, p):
        pl.when(near_when[p])(near_copies[q, p].start)

    def near_arrive(q, p):
        step = OFFSETS[p]
        pl.when((cell + step >= 0) & (cell + step < n_cell))(near_copies[q, p].wait_recv)

    order = list(range(2, n_col)) + [1]
    held = [0]
    for b in bits:
        held += [h ^ b for h in held]

    def cube(view, send, recv, first):
        copies, here = {}, [0]
        for b in bits:
            for h in here:
                slot, index = flip(h), first + len(copies)
                copies[h, b] = remote(view(slot), view(slot), send.at[index], recv.at[index], col=flip(b))
            here = here + [h ^ b for h in here]
        return copies

    def spread(view, send, recv, first):
        return {
            (0, d): remote(view(col), view(col), send.at[first + i], recv.at[first + i], col=flip(d))
            for i, d in enumerate(order)
        }

    def start(copies, h):
        for (source, b), copy in copies.items():
            if source == h:
                copy.start()

    def arrive(copies, h):
        for (source, b), copy in copies.items():
            if source ^ b == h:
                copy.wait_recv()

    own_copies = cube(lambda slot: own.at[slot], own_send, own_recv, 0)
    side_copies = [
        (cube if q < FORWARDED else spread)(
            lambda slot, q=q: beside.at[slot, q], side_send, side_recv, q * (n_col - 1))
        for q in range(CHUNKS)
    ]
    part_copies = [
        remote(ppt, part.at[d - 1], part_send.at[d - 1], part_recv.at[d - 1], col=flip(d))
        for d in range(1, n_col)
    ]
    table_copies = [
        remote(table.at[cell], table.at[cell], table_send.at[d - 1], table_recv.at[d - 1],
               cell=lax.rem(cell + d, n_cell))
        for d in range(1, n_cell)
    ]

    pl.semaphore_wait(barrier, (n_col - 1) + (n_cell - 1))

    near_start(0, 1)
    near_start(0, 2)
    loads["bin"].wait()
    ppt[...] = across(rounded, bin_[...])
    for copy in part_copies:
        copy.start()
    for q in range(1, CHUNKS):
        near_start(q, 1)
        near_start(q, 2)
    start(own_copies, 0)
    for name in ("tile0", "cores", "fsrc", "fcount", "tile1", "bout"):
        loads[name].start()
    for q in range(CHUNKS):
        near_arrive(q, 1)
        near_start(q, 0)
        near_arrive(q, 2)
        near_start(q, 3)

    for copy in part_copies:
        copy.wait_recv()
    total = ppt[...]
    for d in range(1, n_col):
        total = total + part[d - 1]
    table[cell] = total
    for copy in table_copies:
        copy.start()

    def product(tile, buf, chunks):
        places = [(j, q) for j in range(n_col) for q in chunks]
        blocks = jnp.concatenate([buf[j, q] for j, q in places], axis=1)
        columns = jnp.concatenate(
            [tiles[tile, :, j * rows + q * size:j * rows + (q + 1) * size] for j, q in places], axis=1)
        return across(blocks, columns)

    def pick(q):
        near_arrive(q, 0)
        near_arrive(q, 3)
        picked = jnp.zeros(near.shape[2:], BF16)
        for p, step in enumerate(OFFSETS):
            picked = jnp.where(use & (offset == step), near[p, q], picked)
        beside[col, q] = picked
        start(side_copies[q], 0)

    for name in ("count", "offset", "cores", "fsrc", "fcount"):
        loads[name].wait()
    offset = offset_ref[cell]
    use = count_ref[cell] == 2
    rank = cores.shape[1]
    for k in range(0, cores.shape[0], 2):
        flat[:, k * rank:(k + 2) * rank] = jnp.concatenate([cores[k], cores[k + 1]], axis=1)
    arrive(own_copies, bits[0])
    start(own_copies, bits[0])
    for q in range(CHUNKS):
        pick(q)
    for h in held[2:]:
        arrive(own_copies, h)
        start(own_copies, h)
    loads["tile0"].wait()
    acc[...] = product(0, own, range(CHUNKS))
    for h in held[1:-1]:
        for q in range(FORWARDED):
            arrive(side_copies[q], h)
            start(side_copies[q], h)

    for copy in table_copies:
        copy.wait_recv()
    used = fcount_ref[cell]
    picks = []
    for k in range(cores.shape[0]):
        source = table[fsrc_ref[cell, k]]
        picks.append(jnp.where(k < used, source, jnp.zeros_like(source)))
    core = across(
        jnp.concatenate(picks, axis=1), flat[...], precision=lax.Precision.HIGHEST).astype(BF16)

    loads["tile1"].wait()
    loads["bout"].wait()
    for turn in range(2):
        chunks = list(range(turn, CHUNKS, 2))
        for q in chunks:
            for h in held[-1:] if q < FORWARDED else held[1:]:
                arrive(side_copies[q], h)
        acc[...] += product(1, beside, chunks)
        if turn == 0:
            acc[...] += jnp.dot(core, bout[...], preferred_element_type=F32)

    for copy in part_copies + table_copies:
        copy.wait_send()
    for copies in [own_copies] + side_copies:
        for copy in copies.values():
            copy.wait_send()
    for (_, p), copy in near_copies.items():
        pl.when(near_when[p])(copy.wait_send)


def body(
    n_cell, n_col,
    grad, near_tiles, tile_count, near_offset, far_src, far_count, far_cores, basis_out, basis_in
):
    rows, width = grad.shape
    slots, _, clus = near_tiles.shape[1:]
    far, rank = far_cores.shape[1:3]
    size = rows // CHUNKS
    dma = lambda n: pltpu.SemaphoreType.DMA((max(n, 1),))
    hbm = pl.BlockSpec(memory_space=pltpu.HBM)
    out = pl.pallas_call(
        functools.partial(kernel, n_cell, n_col),
        out_shape=pltpu.VMEM((width, rows), F32),
        in_specs=[hbm] * 9,
        out_specs=pl.BlockSpec(memory_space=pltpu.VMEM),
        scratch_shapes=[
            pltpu.SMEM(tile_count.shape, jnp.int32),
            pltpu.SMEM(near_offset.shape, jnp.int32),
            pltpu.SMEM(far_src.shape, jnp.int32),
            pltpu.SMEM(far_count.shape, jnp.int32),
            pltpu.VMEM((width, rows), F32),
            pltpu.VMEM((slots, rows, clus), BF16),
            pltpu.VMEM((far, rank, rank), F32),
            pltpu.VMEM((rank, rows), BF16),
            pltpu.VMEM((rank, rows), BF16),
            pltpu.VMEM((n_col, CHUNKS, width, size), BF16),
            pltpu.VMEM((len(OFFSETS), CHUNKS, width, size), BF16),
            pltpu.VMEM((n_col, CHUNKS, width, size), BF16),
            pltpu.VMEM((width, rank), F32),
            pltpu.VMEM((n_col - 1, width, rank), F32),
            pltpu.VMEM((n_cell, width, rank), F32),
            pltpu.VMEM((rank, far * rank), F32),
            dma(10),
            dma(n_col - 1), dma(n_col - 1),
            dma(len(OFFSETS) * CHUNKS), dma(len(OFFSETS) * CHUNKS),
            dma((n_col - 1) * CHUNKS), dma((n_col - 1) * CHUNKS),
            dma(n_col - 1), dma(n_col - 1),
            dma(n_cell - 1), dma(n_cell - 1),
        ],
        compiler_params=pltpu.CompilerParams(
            collective_id=0, has_side_effects=True, vmem_limit_bytes=56 * 1024 * 1024
        ),
    )(tile_count, near_offset, far_src, far_count, grad.T, near_tiles, far_cores, basis_out.T, basis_in.T)
    return out.T


def solution(mesh):
    placed = (
        P(("chain", "cell", "col"), None),
        P("cell", None, "col", None),
        P(),
        P(),
        P(),
        P(),
        P("cell", None, None, None),
        P(("cell", "col"), None),
        P(("cell", "col"), None),
    )
    return jax.shard_map(
        functools.partial(body, mesh.shape["cell"], mesh.shape["col"]),
        mesh=mesh,
        in_specs=placed,
        out_specs=P(("chain", "cell", "col"), None),
        check_vma=False,
    )
```

```python
import functools

import jax
import jax.numpy as jnp
from jax import lax
from jax.experimental import pallas as pl
from jax.experimental.pallas import tpu as pltpu
from jax.sharding import PartitionSpec as P

MESH = pl.DeviceIdType.MESH
OFFSETS = (-2, -1, 1, 2)
CHUNKS = 4
F32 = jnp.float32
BF16 = jnp.bfloat16


def remote(src, dst, send, recv, **where):
    return pltpu.make_async_remote_copy(
        src_ref=src, dst_ref=dst, send_sem=send, recv_sem=recv, device_id=where, device_id_type=MESH
    )


def across(a, b, **kw):
    return lax.dot_general(a, b, (((1,), (1,)), ((), ())), preferred_element_type=F32, **kw)


def kernel(
    n_cell, n_col,
    count_hbm, offset_hbm, fsrc_hbm, fcount_hbm, grad_hbm, tiles_hbm, cores_hbm, bout_hbm, bin_hbm,
    acc,
    count_ref, offset_ref, fsrc_ref, fcount_ref,
    grad, tiles, cores, bout, bin_,
    own, near, beside, ppt, part, table, flat,
    local_sem, own_send, own_recv, near_send, near_recv, side_send, side_recv,
    part_send, part_recv, table_send, table_recv,
):
    cell = lax.axis_index("cell")
    col = lax.axis_index("col")
    width, rows = grad.shape
    size = rows // CHUNKS
    bits = [1 << b for b in reversed(range(n_col.bit_length() - 1))]

    def flip(d):
        value = col
        for b in bits:
            if d & b:
                value = value + b - 2 * b * lax.rem(value // b, 2)
        return value

    barrier = pltpu.get_barrier_semaphore()
    for d in range(1, n_col):
        pl.semaphore_signal(barrier, inc=1, device_id={"col": flip(d)}, device_id_type=MESH)
    for d in range(1, n_cell):
        pl.semaphore_signal(
            barrier, inc=1, device_id={"cell": lax.rem(cell + d, n_cell)}, device_id_type=MESH
        )

    pairs = {
        "grad": (grad_hbm, grad), "bin": (bin_hbm, bin_),
        "count": (count_hbm, count_ref), "offset": (offset_hbm, offset_ref),
        "fsrc": (fsrc_hbm, fsrc_ref), "fcount": (fcount_hbm, fcount_ref),
        "cores": (cores_hbm.at[0], cores), "tile0": (tiles_hbm.at[0, 0], tiles.at[0]),
        "bout": (bout_hbm, bout), "tile1": (tiles_hbm.at[0, 1], tiles.at[1]),
    }
    loads = {
        name: pltpu.make_async_copy(src, dst, local_sem.at[i])
        for i, (name, (src, dst)) in enumerate(pairs.items())
    }
    for name in ("grad", "bin", "count", "offset", "fsrc", "fcount", "cores", "tile0", "tile1", "bout"):
        loads[name].start()

    for p, step in enumerate(OFFSETS):
        @pl.when((cell + step < 0) | (cell + step >= n_cell))
        def _():
            near[p] = jnp.zeros(near.shape[1:], BF16)
    loads["grad"].wait()
    rounded = grad[...].astype(BF16)
    for q in range(CHUNKS):
        own[col, q] = rounded[:, q * size:(q + 1) * size]

    near_copies, near_when = {}, {}
    for q in range(CHUNKS):
        for p, step in enumerate(OFFSETS):
            index = q * len(OFFSETS) + p
            near_copies[q, p] = remote(
                own.at[col, q], near.at[p, q], near_send.at[index], near_recv.at[index],
                cell=jnp.clip(cell - step, 0, n_cell - 1))
            near_when[p] = (cell - step >= 0) & (cell - step < n_cell)

    def near_start(q, p):
        pl.when(near_when[p])(near_copies[q, p].start)

    def near_arrive(q, p):
        step = OFFSETS[p]
        pl.when((cell + step >= 0) & (cell + step < n_cell))(near_copies[q, p].wait_recv)

    order = list(range(2, n_col)) + [1]

    def spread(buf, send, recv):
        return {
            (d, q): remote(
                buf.at[col, q], buf.at[col, q], send.at[(d - 1) * CHUNKS + q],
                recv.at[(d - 1) * CHUNKS + q], col=flip(d))
            for d in range(1, n_col) for q in range(CHUNKS)
        }

    own_copies, held = {}, [0]
    for b in bits:
        for h in held:
            slot, index = flip(h), len(own_copies)
            own_copies[h, b] = remote(
                own.at[slot], own.at[slot], own_send.at[index], own_recv.at[index], col=flip(b))
        held = held + [h ^ b for h in held]

    side_copies = spread(beside, side_send, side_recv)
    part_copies = [
        remote(ppt, part.at[d - 1], part_send.at[d - 1], part_recv.at[d - 1], col=flip(d))
        for d in range(1, n_col)
    ]
    table_copies = [
        remote(table.at[cell], table.at[cell], table_send.at[d - 1], table_recv.at[d - 1],
               cell=lax.rem(cell + d, n_cell))
        for d in range(1, n_cell)
    ]

    pl.semaphore_wait(barrier, (n_col - 1) + (n_cell - 1))

    for p in (0, 3, 1, 2):
        near_start(0, p)
    loads["bin"].wait()
    ppt[...] = across(rounded, bin_[...])
    for copy in part_copies:
        copy.start()
    for q in range(1, CHUNKS):
        for p in (0, 3, 1, 2):
            near_start(q, p)
        if q == 1:
            for b in bits:
                own_copies[0, b].start()

    for copy in part_copies:
        copy.wait_recv()
    total = ppt[...]
    for d in range(1, n_col):
        total = total + part[d - 1]
    table[cell] = total
    for copy in table_copies:
        copy.start()

    def product(tile, buf, chunks):
        places = [(j, q) for j in range(n_col) for q in chunks]
        blocks = jnp.concatenate([buf[j, q] for j, q in places], axis=1)
        columns = jnp.concatenate(
            [tiles[tile, :, j * rows + q * size:j * rows + (q + 1) * size] for j, q in places], axis=1)
        return across(blocks, columns)

    def pick(q):
        picked = jnp.zeros(near.shape[2:], BF16)
        for p, step in enumerate(OFFSETS):
            near_arrive(q, p)
            picked = jnp.where(use & (offset == step), near[p, q], picked)
        beside[col, q] = picked
        for d in order:
            side_copies[d, q].start()

    for name in ("count", "offset", "cores", "fsrc", "fcount"):
        loads[name].wait()
    offset = offset_ref[cell]
    use = count_ref[cell] == 2
    rank = cores.shape[1]
    for k in range(0, cores.shape[0], 2):
        flat[:, k * rank:(k + 2) * rank] = jnp.concatenate([cores[k], cores[k + 1]], axis=1)
    pick(0)
    for h in held[1:]:
        for (source, b), copy in own_copies.items():
            if source ^ b == h:
                copy.wait_recv()
        for (source, b), copy in own_copies.items():
            if source == h:
                copy.start()
        if h == bits[0]:
            for q in range(1, CHUNKS):
                pick(q)
    loads["tile0"].wait()
    acc[...] = product(0, own, range(CHUNKS))

    def beside_term(chunks):
        for q in chunks:
            for d in order:
                side_copies[d, q].wait_recv()
        acc[...] += product(1, beside, chunks)

    loads["tile1"].wait()
    beside_term(range(CHUNKS // 2))
    for copy in table_copies:
        copy.wait_recv()
    used = fcount_ref[cell]
    picks = []
    for k in range(cores.shape[0]):
        source = table[fsrc_ref[cell, k]]
        picks.append(jnp.where(k < used, source, jnp.zeros_like(source)))
    core = across(
        jnp.concatenate(picks, axis=1), flat[...], precision=lax.Precision.HIGHEST).astype(BF16)

    loads["bout"].wait()
    acc[...] += jnp.dot(core, bout[...], preferred_element_type=F32)
    for q in range(CHUNKS // 2, CHUNKS):
        beside_term([q])

    for copy in part_copies + table_copies:
        copy.wait_send()
    for copy in list(own_copies.values()) + list(side_copies.values()):
        copy.wait_send()
    for (_, p), copy in near_copies.items():
        pl.when(near_when[p])(copy.wait_send)


def body(
    n_cell, n_col,
    grad, near_tiles, tile_count, near_offset, far_src, far_count, far_cores, basis_out, basis_in
):
    rows, width = grad.shape
    slots, _, clus = near_tiles.shape[1:]
    far, rank = far_cores.shape[1:3]
    size = rows // CHUNKS
    dma = lambda n: pltpu.SemaphoreType.DMA((max(n, 1),))
    hbm = pl.BlockSpec(memory_space=pltpu.HBM)
    out = pl.pallas_call(
        functools.partial(kernel, n_cell, n_col),
        out_shape=pltpu.VMEM((width, rows), F32),
        in_specs=[hbm] * 9,
        out_specs=pl.BlockSpec(memory_space=pltpu.VMEM),
        scratch_shapes=[
            pltpu.SMEM(tile_count.shape, jnp.int32),
            pltpu.SMEM(near_offset.shape, jnp.int32),
            pltpu.SMEM(far_src.shape, jnp.int32),
            pltpu.SMEM(far_count.shape, jnp.int32),
            pltpu.VMEM((width, rows), F32),
            pltpu.VMEM((slots, rows, clus), BF16),
            pltpu.VMEM((far, rank, rank), F32),
            pltpu.VMEM((rank, rows), BF16),
            pltpu.VMEM((rank, rows), BF16),
            pltpu.VMEM((n_col, CHUNKS, width, size), BF16),
            pltpu.VMEM((len(OFFSETS), CHUNKS, width, size), BF16),
            pltpu.VMEM((n_col, CHUNKS, width, size), BF16),
            pltpu.VMEM((width, rank), F32),
            pltpu.VMEM((n_col - 1, width, rank), F32),
            pltpu.VMEM((n_cell, width, rank), F32),
            pltpu.VMEM((rank, far * rank), F32),
            dma(10),
            dma(n_col - 1), dma(n_col - 1),
            dma(len(OFFSETS) * CHUNKS), dma(len(OFFSETS) * CHUNKS),
            dma((n_col - 1) * CHUNKS), dma((n_col - 1) * CHUNKS),
            dma(n_col - 1), dma(n_col - 1),
            dma(n_cell - 1), dma(n_cell - 1),
        ],
        compiler_params=pltpu.CompilerParams(
            collective_id=0, has_side_effects=True, vmem_limit_bytes=56 * 1024 * 1024
        ),
    )(tile_count, near_offset, far_src, far_count, grad.T, near_tiles, far_cores, basis_out.T, basis_in.T)
    return out.T


def solution(mesh):
    placed = (
        P(("chain", "cell", "col"), None),
        P("cell", None, "col", None),
        P(),
        P(),
        P(),
        P(),
        P("cell", None, None, None),
        P(("cell", "col"), None),
        P(("cell", "col"), None),
    )
    return jax.shard_map(
        functools.partial(body, mesh.shape["cell"], mesh.shape["col"]),
        mesh=mesh,
        in_specs=placed,
        out_specs=P(("chain", "cell", "col"), None),
        check_vma=False,
    )
```

```python
import functools

import jax
import jax.numpy as jnp
from jax import lax
from jax.experimental import pallas as pl
from jax.experimental.pallas import tpu as pltpu
from jax.sharding import PartitionSpec as P

MESH = pl.DeviceIdType.MESH
OFFSETS = (-2, -1, 1, 2)
CHUNKS = 4
F32 = jnp.float32
BF16 = jnp.bfloat16


def remote(src, dst, send, recv, **where):
    return pltpu.make_async_remote_copy(
        src_ref=src, dst_ref=dst, send_sem=send, recv_sem=recv, device_id=where, device_id_type=MESH
    )


def across(a, b, **kw):
    return lax.dot_general(a, b, (((1,), (1,)), ((), ())), preferred_element_type=F32, **kw)


def kernel(
    n_cell, n_col,
    count_hbm, offset_hbm, fsrc_hbm, fcount_hbm, grad_hbm, tiles_hbm, cores_hbm, bout_hbm, bin_hbm,
    acc,
    count_ref, offset_ref, fsrc_ref, fcount_ref,
    grad, tiles, cores, bout, bin_,
    own, near, beside, ppt, part, table, flat,
    local_sem, own_send, own_recv, near_send, near_recv, side_send, side_recv,
    part_send, part_recv, table_send, table_recv,
):
    cell = lax.axis_index("cell")
    col = lax.axis_index("col")
    width, rows = grad.shape
    size = rows // CHUNKS
    bits = [1 << b for b in reversed(range(n_col.bit_length() - 1))]

    def flip(d):
        value = col
        for b in bits:
            if d & b:
                value = value + b - 2 * b * lax.rem(value // b, 2)
        return value

    barrier = pltpu.get_barrier_semaphore()
    for d in range(1, n_col):
        pl.semaphore_signal(barrier, inc=1, device_id={"col": flip(d)}, device_id_type=MESH)
    for d in range(1, n_cell):
        pl.semaphore_signal(
            barrier, inc=1, device_id={"cell": lax.rem(cell + d, n_cell)}, device_id_type=MESH
        )

    pairs = {
        "grad": (grad_hbm, grad), "bin": (bin_hbm, bin_),
        "count": (count_hbm, count_ref), "offset": (offset_hbm, offset_ref),
        "fsrc": (fsrc_hbm, fsrc_ref), "fcount": (fcount_hbm, fcount_ref),
        "cores": (cores_hbm.at[0], cores), "tile0": (tiles_hbm.at[0, 0], tiles.at[0]),
        "bout": (bout_hbm, bout), "tile1": (tiles_hbm.at[0, 1], tiles.at[1]),
    }
    loads = {
        name: pltpu.make_async_copy(src, dst, local_sem.at[i])
        for i, (name, (src, dst)) in enumerate(pairs.items())
    }
    for name in ("grad", "bin", "count", "offset", "fsrc", "fcount", "cores", "tile0", "tile1", "bout"):
        loads[name].start()

    for p, step in enumerate(OFFSETS):
        @pl.when((cell + step < 0) | (cell + step >= n_cell))
        def _():
            near[p] = jnp.zeros(near.shape[1:], BF16)
    loads["grad"].wait()
    rounded = grad[...].astype(BF16)
    for q in range(CHUNKS):
        own[col, q] = rounded[:, q * size:(q + 1) * size]

    near_copies, near_when = {}, {}
    for q in range(CHUNKS):
        for p, step in enumerate(OFFSETS):
            index = q * len(OFFSETS) + p
            near_copies[q, p] = remote(
                own.at[col, q], near.at[p, q], near_send.at[index], near_recv.at[index],
                cell=jnp.clip(cell - step, 0, n_cell - 1))
            near_when[p] = (cell - step >= 0) & (cell - step < n_cell)

    def near_start(q, p):
        pl.when(near_when[p])(near_copies[q, p].start)

    def near_arrive(q, p):
        step = OFFSETS[p]
        pl.when((cell + step >= 0) & (cell + step < n_cell))(near_copies[q, p].wait_recv)

    order = list(range(2, n_col)) + [1]

    def spread(buf, send, recv):
        return {
            (d, q): remote(
                buf.at[col, q], buf.at[col, q], send.at[(d - 1) * CHUNKS + q],
                recv.at[(d - 1) * CHUNKS + q], col=flip(d))
            for d in range(1, n_col) for q in range(CHUNKS)
        }

    own_copies, held = {}, [0]
    for b in bits:
        for h in held:
            slot, index = flip(h), len(own_copies)
            own_copies[h, b] = remote(
                own.at[slot], own.at[slot], own_send.at[index], own_recv.at[index], col=flip(b))
        held = held + [h ^ b for h in held]

    side_copies = spread(beside, side_send, side_recv)
    part_copies = [
        remote(ppt, part.at[d - 1], part_send.at[d - 1], part_recv.at[d - 1], col=flip(d))
        for d in range(1, n_col)
    ]
    table_copies = [
        remote(table.at[cell], table.at[cell], table_send.at[d - 1], table_recv.at[d - 1],
               cell=lax.rem(cell + d, n_cell))
        for d in range(1, n_cell)
    ]

    pl.semaphore_wait(barrier, (n_col - 1) + (n_cell - 1))

    for p in (0, 3, 1, 2):
        near_start(0, p)
    loads["bin"].wait()
    ppt[...] = across(rounded, bin_[...])
    for copy in part_copies:
        copy.start()
    for q in range(1, CHUNKS):
        for p in (0, 3, 1, 2):
            near_start(q, p)
        if q == 1:
            for b in bits:
                own_copies[0, b].start()

    for copy in part_copies:
        copy.wait_recv()
    total = ppt[...]
    for d in range(1, n_col):
        total = total + part[d - 1]
    table[cell] = total
    for copy in table_copies:
        copy.start()

    def product(tile, buf, chunks):
        places = [(j, q) for j in range(n_col) for q in chunks]
        blocks = jnp.concatenate([buf[j, q] for j, q in places], axis=1)
        columns = jnp.concatenate(
            [tiles[tile, :, j * rows + q * size:j * rows + (q + 1) * size] for j, q in places], axis=1)
        return across(blocks, columns)

    def pick(q):
        picked = jnp.zeros(near.shape[2:], BF16)
        for p, step in enumerate(OFFSETS):
            near_arrive(q, p)
            picked = jnp.where(use & (offset == step), near[p, q], picked)
        beside[col, q] = picked
        for d in order:
            side_copies[d, q].start()

    for name in ("count", "offset", "cores", "fsrc", "fcount"):
        loads[name].wait()
    offset = offset_ref[cell]
    use = count_ref[cell] == 2
    rank = cores.shape[1]
    for k in range(0, cores.shape[0], 2):
        flat[:, k * rank:(k + 2) * rank] = jnp.concatenate([cores[k], cores[k + 1]], axis=1)
    for q in range(CHUNKS // 2):
        pick(q)
    for h in held[1:]:
        for (source, b), copy in own_copies.items():
            if source ^ b == h:
                copy.wait_recv()
        for (source, b), copy in own_copies.items():
            if source == h:
                copy.start()
        if h == bits[0]:
            for q in range(CHUNKS // 2, CHUNKS):
                pick(q)
    loads["tile0"].wait()
    acc[...] = product(0, own, range(CHUNKS))

    def beside_term(chunks):
        for q in chunks:
            for d in order:
                side_copies[d, q].wait_recv()
        acc[...] += product(1, beside, chunks)

    loads["tile1"].wait()
    beside_term(range(CHUNKS // 2))
    for copy in table_copies:
        copy.wait_recv()
    used = fcount_ref[cell]
    picks = []
    for k in range(cores.shape[0]):
        source = table[fsrc_ref[cell, k]]
        picks.append(jnp.where(k < used, source, jnp.zeros_like(source)))
    core = across(
        jnp.concatenate(picks, axis=1), flat[...], precision=lax.Precision.HIGHEST).astype(BF16)

    loads["bout"].wait()
    acc[...] += jnp.dot(core, bout[...], preferred_element_type=F32)
    for q in range(CHUNKS // 2, CHUNKS):
        beside_term([q])

    for copy in part_copies + table_copies:
        copy.wait_send()
    for copy in list(own_copies.values()) + list(side_copies.values()):
        copy.wait_send()
    for (_, p), copy in near_copies.items():
        pl.when(near_when[p])(copy.wait_send)


def body(
    n_cell, n_col,
    grad, near_tiles, tile_count, near_offset, far_src, far_count, far_cores, basis_out, basis_in
):
    rows, width = grad.shape
    slots, _, clus = near_tiles.shape[1:]
    far, rank = far_cores.shape[1:3]
    size = rows // CHUNKS
    dma = lambda n: pltpu.SemaphoreType.DMA((max(n, 1),))
    hbm = pl.BlockSpec(memory_space=pltpu.HBM)
    out = pl.pallas_call(
        functools.partial(kernel, n_cell, n_col),
        out_shape=pltpu.VMEM((width, rows), F32),
        in_specs=[hbm] * 9,
        out_specs=pl.BlockSpec(memory_space=pltpu.VMEM),
        scratch_shapes=[
            pltpu.SMEM(tile_count.shape, jnp.int32),
            pltpu.SMEM(near_offset.shape, jnp.int32),
            pltpu.SMEM(far_src.shape, jnp.int32),
            pltpu.SMEM(far_count.shape, jnp.int32),
            pltpu.VMEM((width, rows), F32),
            pltpu.VMEM((slots, rows, clus), BF16),
            pltpu.VMEM((far, rank, rank), F32),
            pltpu.VMEM((rank, rows), BF16),
            pltpu.VMEM((rank, rows), BF16),
            pltpu.VMEM((n_col, CHUNKS, width, size), BF16),
            pltpu.VMEM((len(OFFSETS), CHUNKS, width, size), BF16),
            pltpu.VMEM((n_col, CHUNKS, width, size), BF16),
            pltpu.VMEM((width, rank), F32),
            pltpu.VMEM((n_col - 1, width, rank), F32),
            pltpu.VMEM((n_cell, width, rank), F32),
            pltpu.VMEM((rank, far * rank), F32),
            dma(10),
            dma(n_col - 1), dma(n_col - 1),
            dma(len(OFFSETS) * CHUNKS), dma(len(OFFSETS) * CHUNKS),
            dma((n_col - 1) * CHUNKS), dma((n_col - 1) * CHUNKS),
            dma(n_col - 1), dma(n_col - 1),
            dma(n_cell - 1), dma(n_cell - 1),
        ],
        compiler_params=pltpu.CompilerParams(
            collective_id=0, has_side_effects=True, vmem_limit_bytes=56 * 1024 * 1024
        ),
    )(tile_count, near_offset, far_src, far_count, grad.T, near_tiles, far_cores, basis_out.T, basis_in.T)
    return out.T


def solution(mesh):
    placed = (
        P(("chain", "cell", "col"), None),
        P("cell", None, "col", None),
        P(),
        P(),
        P(),
        P(),
        P("cell", None, None, None),
        P(("cell", "col"), None),
        P(("cell", "col"), None),
    )
    return jax.shard_map(
        functools.partial(body, mesh.shape["cell"], mesh.shape["col"]),
        mesh=mesh,
        in_specs=placed,
        out_specs=P(("chain", "cell", "col"), None),
        check_vma=False,
    )
```

```python
import functools

import jax
import jax.numpy as jnp
from jax import lax
from jax.experimental import pallas as pl
from jax.experimental.pallas import tpu as pltpu
from jax.sharding import PartitionSpec as P

MESH = pl.DeviceIdType.MESH
OFFSETS = (-2, -1, 1, 2)
CHUNKS = 4
F32 = jnp.float32
BF16 = jnp.bfloat16


def remote(src, dst, send, recv, **where):
    return pltpu.make_async_remote_copy(
        src_ref=src, dst_ref=dst, send_sem=send, recv_sem=recv, device_id=where, device_id_type=MESH
    )


def across(a, b, **kw):
    return lax.dot_general(a, b, (((1,), (1,)), ((), ())), preferred_element_type=F32, **kw)


def kernel(
    n_cell, n_col,
    count_hbm, offset_hbm, fsrc_hbm, fcount_hbm, grad_hbm, tiles_hbm, cores_hbm, bout_hbm, bin_hbm,
    acc,
    count_ref, offset_ref, fsrc_ref, fcount_ref,
    grad, tiles, cores, bout, bin_,
    own, near, beside, ppt, part, table, flat,
    local_sem, own_send, own_recv, near_send, near_recv, side_send, side_recv,
    part_send, part_recv, table_send, table_recv,
):
    cell = lax.axis_index("cell")
    col = lax.axis_index("col")
    width, rows = grad.shape
    size = rows // CHUNKS
    bits = [1 << b for b in reversed(range(n_col.bit_length() - 1))]

    def flip(d):
        value = col
        for b in bits:
            if d & b:
                value = value + b - 2 * b * lax.rem(value // b, 2)
        return value

    barrier = pltpu.get_barrier_semaphore()
    for d in range(1, n_col):
        pl.semaphore_signal(barrier, inc=1, device_id={"col": flip(d)}, device_id_type=MESH)
    for d in range(1, n_cell):
        pl.semaphore_signal(
            barrier, inc=1, device_id={"cell": lax.rem(cell + d, n_cell)}, device_id_type=MESH
        )

    pairs = {
        "grad": (grad_hbm, grad), "bin": (bin_hbm, bin_),
        "count": (count_hbm, count_ref), "offset": (offset_hbm, offset_ref),
        "fsrc": (fsrc_hbm, fsrc_ref), "fcount": (fcount_hbm, fcount_ref),
        "cores": (cores_hbm.at[0], cores), "tile0": (tiles_hbm.at[0, 0], tiles.at[0]),
        "bout": (bout_hbm, bout), "tile1": (tiles_hbm.at[0, 1], tiles.at[1]),
    }
    loads = {
        name: pltpu.make_async_copy(src, dst, local_sem.at[i])
        for i, (name, (src, dst)) in enumerate(pairs.items())
    }
    for name in ("grad", "bin", "count", "offset", "fsrc", "fcount", "cores", "tile0", "tile1", "bout"):
        loads[name].start()

    for p, step in enumerate(OFFSETS):
        @pl.when((cell + step < 0) | (cell + step >= n_cell))
        def _():
            near[p] = jnp.zeros(near.shape[1:], BF16)
    loads["grad"].wait()
    rounded = grad[...].astype(BF16)
    for q in range(CHUNKS):
        own[col, q] = rounded[:, q * size:(q + 1) * size]

    near_copies, near_when = {}, {}
    for q in range(CHUNKS):
        for p, step in enumerate(OFFSETS):
            index = q * len(OFFSETS) + p
            near_copies[q, p] = remote(
                own.at[col, q], near.at[p, q], near_send.at[index], near_recv.at[index],
                cell=jnp.clip(cell - step, 0, n_cell - 1))
            near_when[p] = (cell - step >= 0) & (cell - step < n_cell)

    def near_start(q, p):
        pl.when(near_when[p])(near_copies[q, p].start)

    def near_arrive(q, p):
        step = OFFSETS[p]
        pl.when((cell + step >= 0) & (cell + step < n_cell))(near_copies[q, p].wait_recv)

    order = list(range(2, n_col)) + [1]

    def spread(buf, send, recv):
        return {
            (d, q): remote(
                buf.at[col, q], buf.at[col, q], send.at[(d - 1) * CHUNKS + q],
                recv.at[(d - 1) * CHUNKS + q], col=flip(d))
            for d in range(1, n_col) for q in range(CHUNKS)
        }

    own_copies, held = {}, [0]
    for b in bits:
        for h in held:
            slot, index = flip(h), len(own_copies)
            own_copies[h, b] = remote(
                own.at[slot], own.at[slot], own_send.at[index], own_recv.at[index], col=flip(b))
        held = held + [h ^ b for h in held]

    side_copies = spread(beside, side_send, side_recv)
    part_copies = [
        remote(ppt, part.at[d - 1], part_send.at[d - 1], part_recv.at[d - 1], col=flip(d))
        for d in range(1, n_col)
    ]
    table_copies = [
        remote(table.at[cell], table.at[cell], table_send.at[d - 1], table_recv.at[d - 1],
               cell=lax.rem(cell + d, n_cell))
        for d in range(1, n_cell)
    ]

    pl.semaphore_wait(barrier, (n_col - 1) + (n_cell - 1))

    for p in (0, 3, 1, 2):
        near_start(0, p)
    loads["bin"].wait()
    ppt[...] = across(rounded, bin_[...])
    for copy in part_copies:
        copy.start()
    for q in range(1, CHUNKS):
        for p in (0, 3, 1, 2):
            near_start(q, p)
        if q == CHUNKS - 1:
            for b in bits:
                own_copies[0, b].start()

    for copy in part_copies:
        copy.wait_recv()
    total = ppt[...]
    for d in range(1, n_col):
        total = total + part[d - 1]
    table[cell] = total
    for copy in table_copies:
        copy.start()

    def product(tile, buf, chunks):
        places = [(j, q) for j in range(n_col) for q in chunks]
        blocks = jnp.concatenate([buf[j, q] for j, q in places], axis=1)
        columns = jnp.concatenate(
            [tiles[tile, :, j * rows + q * size:j * rows + (q + 1) * size] for j, q in places], axis=1)
        return across(blocks, columns)

    def pick(q):
        picked = jnp.zeros(near.shape[2:], BF16)
        for p, step in enumerate(OFFSETS):
            near_arrive(q, p)
            picked = jnp.where(use & (offset == step), near[p, q], picked)
        beside[col, q] = picked
        for d in order:
            side_copies[d, q].start()

    for name in ("count", "offset", "cores", "fsrc", "fcount"):
        loads[name].wait()
    offset = offset_ref[cell]
    use = count_ref[cell] == 2
    rank = cores.shape[1]
    for k in range(0, cores.shape[0], 2):
        flat[:, k * rank:(k + 2) * rank] = jnp.concatenate([cores[k], cores[k + 1]], axis=1)
    for q in range(CHUNKS // 2):
        pick(q)
    for h in held[1:]:
        for (source, b), copy in own_copies.items():
            if source ^ b == h:
                copy.wait_recv()
        for (source, b), copy in own_copies.items():
            if source == h:
                copy.start()
        if h == bits[0]:
            for q in range(CHUNKS // 2, CHUNKS):
                pick(q)
    loads["tile0"].wait()
    acc[...] = product(0, own, range(CHUNKS))

    def beside_term(chunks):
        for q in chunks:
            for d in order:
                side_copies[d, q].wait_recv()
        acc[...] += product(1, beside, chunks)

    loads["tile1"].wait()
    beside_term(range(CHUNKS // 2))
    for copy in table_copies:
        copy.wait_recv()
    used = fcount_ref[cell]
    picks = []
    for k in range(cores.shape[0]):
        source = table[fsrc_ref[cell, k]]
        picks.append(jnp.where(k < used, source, jnp.zeros_like(source)))
    core = across(
        jnp.concatenate(picks, axis=1), flat[...], precision=lax.Precision.HIGHEST).astype(BF16)

    loads["bout"].wait()
    acc[...] += jnp.dot(core, bout[...], preferred_element_type=F32)
    for q in range(CHUNKS // 2, CHUNKS):
        beside_term([q])

    for copy in part_copies + table_copies:
        copy.wait_send()
    for copy in list(own_copies.values()) + list(side_copies.values()):
        copy.wait_send()
    for (_, p), copy in near_copies.items():
        pl.when(near_when[p])(copy.wait_send)


def body(
    n_cell, n_col,
    grad, near_tiles, tile_count, near_offset, far_src, far_count, far_cores, basis_out, basis_in
):
    rows, width = grad.shape
    slots, _, clus = near_tiles.shape[1:]
    far, rank = far_cores.shape[1:3]
    size = rows // CHUNKS
    dma = lambda n: pltpu.SemaphoreType.DMA((max(n, 1),))
    hbm = pl.BlockSpec(memory_space=pltpu.HBM)
    out = pl.pallas_call(
        functools.partial(kernel, n_cell, n_col),
        out_shape=pltpu.VMEM((width, rows), F32),
        in_specs=[hbm] * 9,
        out_specs=pl.BlockSpec(memory_space=pltpu.VMEM),
        scratch_shapes=[
            pltpu.SMEM(tile_count.shape, jnp.int32),
            pltpu.SMEM(near_offset.shape, jnp.int32),
            pltpu.SMEM(far_src.shape, jnp.int32),
            pltpu.SMEM(far_count.shape, jnp.int32),
            pltpu.VMEM((width, rows), F32),
            pltpu.VMEM((slots, rows, clus), BF16),
            pltpu.VMEM((far, rank, rank), F32),
            pltpu.VMEM((rank, rows), BF16),
            pltpu.VMEM((rank, rows), BF16),
            pltpu.VMEM((n_col, CHUNKS, width, size), BF16),
            pltpu.VMEM((len(OFFSETS), CHUNKS, width, size), BF16),
            pltpu.VMEM((n_col, CHUNKS, width, size), BF16),
            pltpu.VMEM((width, rank), F32),
            pltpu.VMEM((n_col - 1, width, rank), F32),
            pltpu.VMEM((n_cell, width, rank), F32),
            pltpu.VMEM((rank, far * rank), F32),
            dma(10),
            dma(n_col - 1), dma(n_col - 1),
            dma(len(OFFSETS) * CHUNKS), dma(len(OFFSETS) * CHUNKS),
            dma((n_col - 1) * CHUNKS), dma((n_col - 1) * CHUNKS),
            dma(n_col - 1), dma(n_col - 1),
            dma(n_cell - 1), dma(n_cell - 1),
        ],
        compiler_params=pltpu.CompilerParams(
            collective_id=0, has_side_effects=True, vmem_limit_bytes=56 * 1024 * 1024
        ),
    )(tile_count, near_offset, far_src, far_count, grad.T, near_tiles, far_cores, basis_out.T, basis_in.T)
    return out.T


def solution(mesh):
    placed = (
        P(("chain", "cell", "col"), None),
        P("cell", None, "col", None),
        P(),
        P(),
        P(),
        P(),
        P("cell", None, None, None),
        P(("cell", "col"), None),
        P(("cell", "col"), None),
    )
    return jax.shard_map(
        functools.partial(body, mesh.shape["cell"], mesh.shape["col"]),
        mesh=mesh,
        in_specs=placed,
        out_specs=P(("chain", "cell", "col"), None),
        check_vma=False,
    )
```
